128 devices in a mesh: rep: 4 (over y), fsdp: 32 (over z, x, core).
Axes of the slice: x: 4, y: 4, z: 4, core: 2. Of those that a mesh axis runs over, the one named last changes fastest.
Arguments:
- grads: bfloat16 [4, 256, 512, 512], P('rep', None, 'fsdp'), may hold values from -40 to 40
- owner: int32 [256], replicated, may hold values from 0 to 31, as said below
- factor_left: float32 [384, 512, 512], P(('rep', 'fsdp')), may hold values from -0.6 to 0.6
- factor_right: float32 [384, 512, 512], P(('rep', 'fsdp')), may hold values from -0.6 to 0.6
- precond_left: bfloat16 [384, 512, 512], P(('rep', 'fsdp')), may hold values from -0.125 to 1.625
- precond_right: bfloat16 [384, 512, 512], P(('rep', 'fsdp')), may hold values from -0.125 to 1.625
Outputs:
- new_left: float32 [384, 512, 512], P(('rep', 'fsdp'))
- new_right: float32 [384, 512, 512], P(('rep', 'fsdp'))
- direction: bfloat16 [256, 512, 512], P(None, 'fsdp')
The draws below stay inside these ranges and needn't reach their ends.
Inputs may be any that keep to these rules, and one draw needn't show every extreme that they name: Each owner column holds at most 12 blocks, and some column exactly that many.
All inputs are finite; a program needn't handle non-finite values.
Results may differ from the reference program's by a relative error of at most 0.017.
Values may be sent and summed in bfloat16 or wider, within the bound.
No kernel may reach another device: no remote copies, remote signals or barrier semaphores. Data moves between devices by JAX's collectives and lax.ppermute only.
A program may use at most 128 MiB of HBM per device.

```python
import jax
import jax.numpy as jnp
from jax import lax

BS = 512
CAPR = 3
REPLICAS = 4
COLUMNS = 32
BLOCKS = 256
SLOTS = 384


def precond_matrix(key):
    first, second = jax.random.split(key, 2)
    values = jnp.clip(jax.random.normal(first, (SLOTS, BS, BS), jnp.float32), -4.0, 4.0)
    mixed = (values + jnp.swapaxes(values, 1, 2)) * (0.5 / jnp.sqrt(2.0 * BS))
    mixed = jnp.clip(mixed, -0.125, 0.125)
    diag_scale = jnp.exp(jax.random.uniform(second, (SLOTS, BS, 1), jnp.float32, jnp.log(0.5), jnp.log(1.5)))
    row_ids = lax.broadcasted_iota(jnp.int32, (1, BS, BS), 1)
    col_ids = lax.broadcasted_iota(jnp.int32, (1, BS, BS), 2)
    identity = (row_ids == col_ids).astype(jnp.float32)
    return (mixed + diag_scale * identity).astype(jnp.bfloat16)


def draw_precond_left(key, part):
    key = jax.random.fold_in(key, 21)
    return precond_matrix(key)


def draw_precond_right(key, part):
    key = jax.random.fold_in(key, 37)
    return precond_matrix(key)


def draw_grads(key, part):
    key = jax.random.fold_in(key, 11)
    first, second, third = jax.random.split(key, 3)
    row_scale = jnp.exp(jax.random.uniform(first, (1, BLOCKS, BS, 1), jnp.float32, -1.15, 1.15))
    col_scale = jnp.exp(jax.random.uniform(second, (1, BLOCKS, 1, BS), jnp.float32, -1.15, 1.15))
    values = jnp.clip(jax.random.normal(third, (REPLICAS, BLOCKS, BS, BS), jnp.float32), -4.0, 4.0)
    return (values * row_scale * col_scale).astype(jnp.bfloat16)


def draw_owner(key, part):
    key = jax.random.fold_in(key, 5)
    first, second, third = jax.random.split(key, 3)
    capacity = REPLICAS * CAPR
    total = COLUMNS * capacity
    scores = jax.random.permutation(first, total).astype(jnp.int32)
    chosen = jax.random.randint(second, (), 0, COLUMNS)
    column_ids = jnp.arange(total, dtype=jnp.int32) // capacity
    scores = scores + jnp.where(column_ids == chosen, total, 0).astype(jnp.int32)
    top_values, top_slots = lax.top_k(scores, BLOCKS)
    owners = (top_slots // capacity).astype(jnp.int32)
    return jax.random.permutation(third, owners).astype(jnp.int32)


def block_levels(own_key, dims, shards, least, high):
    level = 1.0
    for axis_at, blocks in shards:
        draws = jax.random.uniform(jax.random.fold_in(jax.random.fold_in(own_key, 6), axis_at), (blocks,), jnp.float32, least / len(shards), high / len(shards))
        level = level * jnp.repeat(jnp.exp(draws), dims[axis_at] // blocks).reshape((-1,) + (1,) * (len(dims) - 1 - axis_at))
    return level


def scatter_about(own_key, shape, deviation, most, shards=(), kind=jnp.bfloat16):
    values = jax.random.normal(own_key, shape, jnp.float32) * deviation
    if len(shards) > 0:
        values = block_levels(own_key, shape, shards, -0.22, 0.18) * values
    return jnp.clip(values, min=-most, max=most).astype(kind)


def setup_inputs(seed: int = 0) -> dict:
    seeds = jax.random.split(jax.random.key(seed), 7)
    grads = draw_grads(jax.random.fold_in(seeds[6], 71), 0)
    owner = draw_owner(jax.random.fold_in(seeds[6], 71), 0)
    factor_left = scatter_about(seeds[2], (SLOTS, BS, BS), 0.1, 0.6, ((0, 128),), jnp.float32)
    factor_right = scatter_about(seeds[3], (SLOTS, BS, BS), 0.1, 0.6, ((0, 128),), jnp.float32)
    precond_left = draw_precond_left(jax.random.fold_in(seeds[6], 71), 0)
    precond_right = draw_precond_right(jax.random.fold_in(seeds[6], 71), 0)
    return dict(grads=grads, owner=owner, factor_left=factor_left, factor_right=factor_right, precond_left=precond_left, precond_right=precond_right)


epsilon = 1e-06
decay_rate = 0.9

def reference(grads, owner, factor_left, factor_right, precond_left, precond_right):
    summed = lax.optimization_barrier(jnp.sum(grads.astype(jnp.float32), axis=0))
    position = jnp.arange(BLOCKS, dtype=jnp.int32)
    same_owner = (owner[:, None] == owner[None, :]) & (position[None, :] < position[:, None])
    col_rank = lax.optimization_barrier(jnp.sum(same_owner.astype(jnp.int32), axis=1))
    slot_of = ((col_rank % REPLICAS * COLUMNS + owner) * CAPR + col_rank // REPLICAS).astype(jnp.int32)
    block_of = jnp.full((SLOTS,), BLOCKS, jnp.int32).at[slot_of].set(position)
    padded = jnp.concatenate([summed, jnp.zeros((1, BS, BS), jnp.float32)], axis=0)

    def one_slot(items):
        left, right, pleft, pright, index = items
        block = lax.dynamic_index_in_dim(padded, index.astype(jnp.int32), 0, keepdims=False)
        left_gram = jnp.dot(block, block.T, precision=lax.Precision.HIGHEST)
        right_gram = jnp.dot(block.T, block, precision=lax.Precision.HIGHEST)
        out_left = decay_rate * left + (1.0 - decay_rate) / BS * left_gram
        out_right = decay_rate * right + (1.0 - decay_rate) / BS * right_gram
        block_low = block.astype(jnp.bfloat16)
        left_applied = jnp.dot(pleft, block_low, preferred_element_type=jnp.float32).astype(jnp.bfloat16)
        preconditioned = jnp.dot(left_applied, pright, preferred_element_type=jnp.float32)
        grafting = jnp.sqrt((jnp.mean(block * block) + epsilon) / (jnp.mean(preconditioned * preconditioned) + epsilon))
        return (out_left, out_right, (preconditioned * grafting).astype(jnp.bfloat16))
    new_left, new_right, shaped = lax.map(one_slot, (factor_left, factor_right, precond_left, precond_right, block_of))
    direction = jnp.take(shaped, slot_of, axis=0)
    return (new_left, new_right, direction)
```

```python
import functools

import jax
import jax.numpy as jnp
from jax import lax
from jax.experimental import pallas as pl
from jax.experimental.pallas import tpu as pltpu
from jax.sharding import PartitionSpec as P

epsilon = 1e-06
decay_rate = 0.9

ANY = pl.BlockSpec(memory_space=pl.ANY)
SMEM = pl.BlockSpec(memory_space=pltpu.SMEM)
VMEM = pl.BlockSpec(memory_space=pltpu.VMEM)
F32 = jnp.float32
LIMIT = 48 * 1024 * 1024


def params():
    return pltpu.CompilerParams(vmem_limit_bytes=LIMIT)


def cost(nbytes, flops=0):
    return pl.CostEstimate(flops=flops, bytes_accessed=nbytes, transcendentals=0)


def fetch(rows, table, start, count, into, first, sem, last):
    def one(j, _):
        block = jnp.minimum(table[start + j], last)
        pltpu.make_async_copy(rows.at[block], into.at[first + j], sem).start()
        return 0

    lax.fori_loop(0, count, one, 0, unroll=4)


def drain(into, sem):
    pltpu.make_async_copy(into, into, sem).wait()


def first_kernel(size, table, rows, low, high, sems):
    last = rows.shape[0] - 1
    half = size // 2
    fetch(rows, table, 2 * size, half, low, 0, sems.at[0], last)
    fetch(rows, table, 2 * size + half, half, high, 0, sems.at[1], last)
    drain(low, sems.at[0])
    drain(high, sems.at[1])


def second_kernel(size, table, rows, got_low, got_high, up, down, sems):
    last = rows.shape[0] - 1
    half = size // 2
    fetch(rows, table, size, size, up, 0, sems.at[0], last)
    fetch(rows, table, 3 * size, size, down, 0, sems.at[1], last)
    drain(up, sems.at[0])

    def add_low(j, _):
        up[j] = (up[j].astype(F32) + got_low[j].astype(F32)).astype(up.dtype)
        return 0

    lax.fori_loop(0, half, add_low, 0, unroll=4)
    drain(down, sems.at[1])

    def add_high(j, _):
        k = half + j
        down[k] = (down[k].astype(F32) + got_high[j].astype(F32)).astype(down.dtype)
        return 0

    lax.fori_loop(0, half, add_high, 0, unroll=4)


def third_kernel(size, base, table, place, rows, from_up, from_down, out, own, sem):
    last = rows.shape[0] - 1
    fetch(rows, table, 0, size, own, 0, sem, last)
    out[...] = jnp.zeros_like(out)
    drain(own, sem)

    def one(j, _):
        block = table[j]

        @pl.when(block <= last)
        def _():
            where = place[block]
            total = own[j].astype(F32) + from_up[j].astype(F32) + from_down[j].astype(F32)
            out[where % 32, where // 32 - base] = total.astype(out.dtype)

        return 0

    lax.fori_loop(0, size, one, 0)


def pack_kernel(size, base, last, table, place, returned, out, sem):
    def one(j, _):
        block = jnp.minimum(table[j], last)
        where = place[block]
        layer = jnp.maximum(where // 32 - base, 0)
        pltpu.make_async_copy(returned.at[where % 32, layer], out.at[j], sem).start()
        return 0

    lax.fori_loop(0, size, one, 0, unroll=4)
    drain(out, sem)


def place_kernel(plan, last, table, *refs):
    sources, out, sem = refs[: len(plan)], refs[-2], refs[-1]

    def each(act):
        for source, (start, count, shift) in zip(sources, plan):

            def one(j, _, source=source, start=start, shift=shift):
                block = table[start + j]

                @pl.when(block <= last)
                def _():
                    act(pltpu.make_async_copy(source.at[shift + j], out.at[block], sem))

                return 0

            lax.fori_loop(0, count, one, 0)

    each(lambda copy: copy.start())
    each(lambda copy: copy.wait())


def apply_kernel(held, left, right, shaped):
    order = left.shape[-1]
    block = held[...].reshape(order, order)
    applied = jnp.dot(left[0], block, preferred_element_type=F32).astype(jnp.bfloat16)
    product = jnp.dot(applied, right[0], preferred_element_type=F32)
    wide = block.astype(F32)
    count = order * order
    held_power = jnp.sum(wide * wide) / count
    power = jnp.sum(product * product) / count
    scale = jnp.sqrt((held_power + epsilon) / (power + epsilon))
    shaped[...] = (product * scale).astype(jnp.bfloat16).reshape(shaped.shape)


def gram_kernel(held_first, held_rest, left, right, new_left, new_right):
    order = left.shape[-1]
    block = jnp.where(pl.program_id(0) == 0, held_first[...], held_rest[...]).reshape(order, order)
    weight = (1.0 - decay_rate) / order
    left_gram = lax.dot_general(block, block, (((1,), (1,)), ((), ())), preferred_element_type=F32)
    right_gram = lax.dot_general(block, block, (((0,), (0,)), ((), ())), preferred_element_type=F32)
    new_left[0] = decay_rate * left[0] + weight * left_gram
    new_right[0] = decay_rate * right[0] + weight * right_gram


def local(grads, owner, factor_left, factor_right, precond_left, precond_right):
    rows = grads[0]
    blocks, band, width = rows.shape
    columns = lax.axis_size("fsdp")
    replicas = lax.axis_size("rep")
    my_rep = lax.axis_index("rep")
    slots = factor_left.shape[0]
    last = blocks - 1
    up_pairs = [(i, (i + 1) % replicas) for i in range(replicas)]
    down_pairs = [(i, (i - 1) % replicas) for i in range(replicas)]

    position = jnp.arange(blocks, dtype=jnp.int32)
    earlier = position[None, :] < position[:, None]
    same_owner = (owner[:, None] == owner[None, :]) & earlier
    col_rank = jnp.sum(same_owner.astype(jnp.int32), axis=1)
    rep_of = col_rank % replicas
    local_slot = col_rank // replicas
    relative = (rep_of - my_rep) % replicas
    place = local_slot * columns + owner

    def listed(key, size):
        hits = key[None, :] == jnp.arange(size, dtype=jnp.int32)[:, None]
        return jnp.min(jnp.where(hits, position[None, :], blocks), axis=1)

    size_first = columns
    table_first = listed(jnp.where(local_slot == 0, relative * columns + owner, -1), replicas * columns)
    size_rest = 56
    in_rest = local_slot > 0
    same_list = (rep_of[:, None] == rep_of[None, :]) & in_rest[None, :] & earlier
    in_list = jnp.sum(same_list.astype(jnp.int32), axis=1)
    table_rest = listed(jnp.where(in_rest, relative * size_rest + in_list, -1), replicas * size_rest)

    def piece(count):
        return jax.ShapeDtypeStruct((count, band, width), jnp.bfloat16)

    def nbytes(count):
        return count * band * width * 2

    def sums(table, size, base, depth):
        half = size // 2
        low, high = pl.pallas_call(
            functools.partial(first_kernel, size),
            out_shape=(piece(half), piece(half)),
            in_specs=[SMEM, ANY],
            out_specs=(ANY, ANY),
            scratch_shapes=[pltpu.SemaphoreType.DMA((2,))],
            compiler_params=params(),
            cost_estimate=cost(nbytes(2 * size)),
        )(table, rows)
        got_low = lax.ppermute(low, "rep", up_pairs)
        got_high = lax.ppermute(high, "rep", down_pairs)
        up, down = pl.pallas_call(
            functools.partial(second_kernel, size),
            out_shape=(piece(size), piece(size)),
            in_specs=[SMEM, ANY, VMEM, VMEM],
            out_specs=(VMEM, VMEM),
            scratch_shapes=[pltpu.SemaphoreType.DMA((2,))],
            compiler_params=params(),
            cost_estimate=cost(nbytes(5 * size)),
        )(table, rows, got_low, got_high)
        from_up = lax.ppermute(up, "rep", up_pairs)
        from_down = lax.ppermute(down, "rep", down_pairs)
        return pl.pallas_call(
            functools.partial(third_kernel, size, base),
            out_shape=jax.ShapeDtypeStruct((columns, depth, band, width), jnp.bfloat16),
            in_specs=[SMEM, SMEM, ANY, VMEM, VMEM],
            out_specs=VMEM,
            scratch_shapes=[pltpu.VMEM((size, band, width), jnp.bfloat16), pltpu.SemaphoreType.DMA],
            compiler_params=params(),
            cost_estimate=cost(nbytes(5 * size)),
        )(table, place, rows, from_up, from_down)

    def exchange(x):
        return lax.all_to_all(x, "fsdp", split_axis=0, concat_axis=0, tiled=True)

    def applied(held, base, depth):
        order = factor_left.shape[1]
        strip = pl.BlockSpec((columns, 1, band, width), lambda s: (0, s, 0, 0))
        matrix = pl.BlockSpec((1, order, order), lambda s: (s + base, 0, 0))
        return pl.pallas_call(
            apply_kernel,
            grid=(depth,),
            out_shape=jax.ShapeDtypeStruct(held.shape, jnp.bfloat16),
            in_specs=[strip, matrix, matrix],
            out_specs=strip,
            compiler_params=params(),
            cost_estimate=cost(depth * 4 * order * order * 2, depth * 4 * order**3),
        )(held, precond_left, precond_right)

    def spread(chunk):
        half = chunk.shape[0] // 2
        below = lax.ppermute(chunk, "rep", up_pairs)
        above = lax.ppermute(chunk, "rep", down_pairs)
        return below, above, half

    def placed(table, plan, sources, out):
        extra = [] if out is None else [out]

        def kernel(*refs):
            place_kernel(plan, last, *refs[: 1 + len(plan)], *refs[-2:])

        return pl.pallas_call(
            kernel,
            out_shape=piece(blocks),
            in_specs=[SMEM] + [ANY] * (len(sources) + len(extra)),
            out_specs=ANY,
            scratch_shapes=[pltpu.SemaphoreType.DMA],
            input_output_aliases={} if out is None else {1 + len(sources): 0},
            compiler_params=params(),
            cost_estimate=cost(nbytes(2 * sum(p[1] for p in plan))),
        )(table, *sources, *extra)

    sent_first = sums(table_first, size_first, 0, 1)
    held_first = exchange(sent_first)
    sent_rest = sums(table_rest, size_rest, 1, slots - 1)
    back_first = exchange(applied(held_first, 0, 1))
    held_rest = exchange(sent_rest)
    back_rest = exchange(applied(held_rest, 1, slots - 1))

    own_first = back_first.reshape(columns, band, width)
    below_first, above_first, half_first = spread(own_first)
    far_low_first = lax.ppermute(below_first[:half_first], "rep", up_pairs)
    far_high_first = lax.ppermute(above_first[half_first:], "rep", down_pairs)

    own_rest = pl.pallas_call(
        functools.partial(pack_kernel, size_rest, 1, last),
        out_shape=piece(size_rest),
        in_specs=[SMEM, SMEM, ANY],
        out_specs=ANY,
        scratch_shapes=[pltpu.SemaphoreType.DMA],
        compiler_params=params(),
        cost_estimate=cost(nbytes(2 * size_rest)),
    )(table_rest, place, back_rest)
    below_rest, above_rest, half_rest = spread(own_rest)
    far_low_rest = lax.ppermute(below_rest[:half_rest], "rep", up_pairs)
    far_high_rest = lax.ppermute(above_rest[half_rest:], "rep", down_pairs)

    order = factor_left.shape[1]
    matrix = pl.BlockSpec((1, order, order), lambda s: (s, 0, 0))
    new_left, new_right = pl.pallas_call(
        gram_kernel,
        grid=(slots,),
        out_shape=(
            jax.ShapeDtypeStruct(factor_left.shape, F32),
            jax.ShapeDtypeStruct(factor_right.shape, F32),
        ),
        in_specs=[
            pl.BlockSpec((columns, 1, band, width), lambda s: (0, 0, 0, 0)),
            pl.BlockSpec((columns, 1, band, width), lambda s: (0, jnp.maximum(s - 1, 0), 0, 0)),
            matrix,
            matrix,
        ],
        out_specs=(matrix, matrix),
        compiler_params=params(),
        cost_estimate=cost(slots * 18 * order * order, slots * 4 * order**3),
    )(held_first, held_rest, factor_left, factor_right)

    def all_plan(size):
        half = size // 2
        return [(0, size, 0), (size, size, 0), (3 * size, size, 0), (2 * size, half, 0), (2 * size + half, half, 0)]

    plan_first, plan_rest = all_plan(size_first), all_plan(size_rest)
    direction = placed(
        table_first, plan_first, [own_first, above_first, below_first, far_low_first, far_high_first], None
    )
    direction = placed(table_rest, plan_rest[:3], [own_rest, above_rest, below_rest], direction)
    direction = placed(table_rest, plan_rest[3:], [far_low_rest, far_high_rest], direction)
    return (new_left, new_right, direction)


def solution(mesh):
    placed = (
        P("rep", None, "fsdp", None),
        P(),
        P(("rep", "fsdp"), None, None),
        P(("rep", "fsdp"), None, None),
        P(("rep", "fsdp"), None, None),
        P(("rep", "fsdp"), None, None),
    )
    return jax.shard_map(
        local,
        mesh=mesh,
        in_specs=placed,
        out_specs=(
            P(("rep", "fsdp"), None, None),
            P(("rep", "fsdp"), None, None),
            P(None, "fsdp", None),
        ),
        check_vma=False,
    )
```

```python
import functools

import jax
import jax.numpy as jnp
from jax import lax
from jax.experimental import pallas as pl
from jax.experimental.pallas import tpu as pltpu
from jax.sharding import PartitionSpec as P

epsilon = 1e-06
decay_rate = 0.9

ANY = pl.BlockSpec(memory_space=pl.ANY)
HBM = pl.BlockSpec(memory_space=pltpu.HBM)
SMEM = pl.BlockSpec(memory_space=pltpu.SMEM)
VMEM = pl.BlockSpec(memory_space=pltpu.VMEM)
F32 = jnp.float32
MIB = 1024 * 1024


def cost(nbytes, flops=0):
    return pl.CostEstimate(flops=flops, bytes_accessed=nbytes, transcendentals=0)


def fetch(rows, table, start, count, into, sem, last):
    def one(j, _):
        block = jnp.minimum(table[start + j], last)
        pltpu.make_async_copy(rows.at[block], into.at[j], sem).start()
        return 0

    lax.fori_loop(0, count, one, 0, unroll=4)


def first_kernel(size, table, rows, low, high, sems):
    last = rows.shape[0] - 1
    half = size // 2
    fetch(rows, table, 2 * size, half, low, sems.at[0], last)
    fetch(rows, table, 2 * size + half, half, high, sems.at[1], last)
    pltpu.make_async_copy(low, low, sems.at[0]).wait()
    pltpu.make_async_copy(high, high, sems.at[1]).wait()


def lay_kernel(plan, table, rows):
    last = rows.shape[0] - 1
    for start, out in plan:

        def one(j, _, start=start, out=out):
            out[j] = rows[jnp.minimum(table[start + j], last)]
            return 0

        lax.fori_loop(0, out.shape[0], one, 0, unroll=4)


def second_kernel(got_low, got_high, low_rows, high_rows, low, high):
    def one(j, _):
        low[j] = (low_rows[j].astype(F32) + got_low[j].astype(F32)).astype(low.dtype)
        high[j] = (high_rows[j].astype(F32) + got_high[j].astype(F32)).astype(high.dtype)
        return 0

    lax.fori_loop(0, low.shape[0], one, 0, unroll=4)


def second_whole_kernel(got_low, got_high, up_rows, down_rows, up, down):
    half = got_low.shape[0]

    def one(j, _):
        k = half + j
        up[j] = (up_rows[j].astype(F32) + got_low[j].astype(F32)).astype(up.dtype)
        down[k] = (down_rows[k].astype(F32) + got_high[j].astype(F32)).astype(down.dtype)
        return 0

    lax.fori_loop(0, half, one, 0, unroll=4)


def third_first_kernel(size, last, table, own, up_low, up_high, down_low, down_high, out):
    half = size // 2
    for first, from_up, from_down in ((0, up_low, down_low), (half, up_high, down_high)):

        def one(k, _, first=first, from_up=from_up, from_down=from_down):
            j = first + k
            total = own[j].astype(F32) + from_up[k].astype(F32) + from_down[k].astype(F32)
            out[j, 0] = jnp.where(table[j] <= last, total, 0.0).astype(out.dtype)
            return 0

        lax.fori_loop(0, half, one, 0, unroll=4)


def third_kernel(size, base, last, table, place, own, from_up, from_down, back, out):
    depth = out.shape[1]

    def clear(j, _):
        for part in range(depth - 1):
            out[j, part] = jnp.zeros_like(out[j, part])
        out[j, depth - 1] = back[j, 0]
        return 0

    lax.fori_loop(0, out.shape[0], clear, 0, unroll=4)
    count = lax.fori_loop(0, size, lambda j, n: n + jnp.where(table[j] <= last, 1, 0), 0, unroll=8)

    def some(i, _):
        for lane in range(4):
            j = jnp.minimum(4 * i + lane, count - 1)
            where = place[table[j]]
            total = own[j].astype(F32) + from_up[j].astype(F32) + from_down[j].astype(F32)
            out[where & 31, (where >> 5) - base] = total.astype(out.dtype)
        return 0

    lax.fori_loop(0, (count + 3) // 4, some, 0)


def pack_kernel(half, base, last, table, place, returned, low, high):
    for first, out in ((0, low), (half, high)):

        def one(j, _, first=first, out=out):
            where = place[jnp.minimum(table[first + j], last)]
            layer = jnp.maximum((where >> 5) - base, 0)
            out[j] = returned[where & 31, layer]
            return 0

        lax.fori_loop(0, half, one, 0, unroll=4)


def take_kernel(part, mixed, low, high):
    half = low.shape[0]

    def one(j, _):
        low[j] = mixed[j, part]
        high[j] = mixed[half + j, part]
        return 0

    lax.fori_loop(0, half, one, 0, unroll=4)


def place_kernel(plan, last, table, *refs):
    sources, out, sem = refs[: len(plan)], refs[-2], refs[-1]

    def each(act):
        for source, (start, count, shift) in zip(sources, plan):

            def one(j, _, source=source, start=start, shift=shift):
                block = table[start + j]

                @pl.when(block <= last)
                def _():
                    act(pltpu.make_async_copy(source.at[shift + j], out.at[block], sem))

                return 0

            lax.fori_loop(0, count, one, 0)

    each(lambda copy: copy.start())
    each(lambda copy: copy.wait())


def apply_kernel(held, left, right, shaped):
    order = left.shape[-1]
    block = held[...].reshape(order, order)
    applied = jnp.dot(left[0], block, preferred_element_type=F32).astype(jnp.bfloat16)
    product = jnp.dot(applied, right[0], preferred_element_type=F32)
    wide = block.astype(F32)
    count = order * order
    held_power = jnp.sum(wide * wide) / count
    power = jnp.sum(product * product) / count
    scale = jnp.sqrt((held_power + epsilon) / (power + epsilon))
    shaped[...] = (product * scale).astype(jnp.bfloat16).reshape(shaped.shape)


def gram_kernel(held_first, held_rest, left, right, new_left, new_right):
    order = left.shape[-1]
    block = jnp.where(pl.program_id(0) == 0, held_first[...], held_rest[...]).reshape(order, order)
    weight = (1.0 - decay_rate) / order
    left_gram = lax.dot_general(block, block, (((1,), (1,)), ((), ())), preferred_element_type=F32)
    right_gram = lax.dot_general(block, block, (((0,), (0,)), ((), ())), preferred_element_type=F32)
    new_left[0] = decay_rate * left[0] + weight * left_gram
    new_right[0] = decay_rate * right[0] + weight * right_gram


def local(grads, owner, factor_left, factor_right, precond_left, precond_right):
    rows = grads[0]
    blocks, band, width = rows.shape
    columns = lax.axis_size("fsdp")
    replicas = lax.axis_size("rep")
    my_rep = lax.axis_index("rep")
    slots = factor_left.shape[0]
    last = blocks - 1
    up_pairs = [(i, (i + 1) % replicas) for i in range(replicas)]
    down_pairs = [(i, (i - 1) % replicas) for i in range(replicas)]
    far_pairs = [(i, (i + 2) % replicas) for i in range(replicas)]

    position = jnp.arange(blocks, dtype=jnp.int32)
    earlier = position[None, :] < position[:, None]
    same_owner = (owner[:, None] == owner[None, :]) & earlier
    col_rank = jnp.sum(same_owner.astype(jnp.int32), axis=1)
    rep_of = col_rank % replicas
    local_slot = col_rank // replicas
    relative = (rep_of - my_rep) % replicas
    place = local_slot * columns + owner

    def listed(key, size):
        hits = key[None, :] == jnp.arange(size, dtype=jnp.int32)[:, None]
        return jnp.min(jnp.where(hits, position[None, :], blocks), axis=1)

    size_first = columns
    by_column = relative * columns + owner
    table_first = listed(jnp.where(local_slot == 0, by_column, -1), replicas * columns)

    def packed(member, size):
        same_list = (rep_of[:, None] == rep_of[None, :]) & member[None, :] & earlier
        in_list = jnp.sum(same_list.astype(jnp.int32), axis=1)
        return listed(jnp.where(member, relative * size + in_list, -1), replicas * size)

    size_rest = 56
    table_rest = packed(local_slot > 0, size_rest)

    def piece(*count):
        return jax.ShapeDtypeStruct((*count, band, width), jnp.bfloat16)

    def nbytes(count):
        return count * band * width * 2

    token = jax.ShapeDtypeStruct((8, 128), F32)

    def call(kernel, results, operands, specs, out_specs, scratch=(), after=(), moved=0, flops=0, grid=None, aliases=None, limit=16):
        count, late = len(operands), len(after)
        n_out = len(results)
        small = pl.BlockSpec((8, 128), lambda *_: (0, 0)) if grid else VMEM

        def body(*refs):
            outs = refs[count + late : count + late + n_out]
            mark = refs[count + late + n_out]
            mark[...] = jnp.zeros_like(mark)
            kernel(*refs[:count], *outs, *refs[count + late + n_out + 1 :])

        extra = {} if grid is None else {"grid": grid}
        return pl.pallas_call(
            body,
            out_shape=(*results, token),
            in_specs=list(specs) + [ANY] * late,
            out_specs=(*out_specs, small),
            scratch_shapes=list(scratch),
            input_output_aliases=aliases or {},
            compiler_params=pltpu.CompilerParams(vmem_limit_bytes=limit * MIB),
            cost_estimate=pl.CostEstimate(flops=flops, bytes_accessed=moved, transcendentals=0),
            **extra,
        )(*operands, *after)

    def tip(x):
        return x[0, :16, :128]

    def both_ways(up, down):
        return lax.ppermute(up, "rep", up_pairs), lax.ppermute(down, "rep", down_pairs)

    def half_plan(size):
        return [(relative * size + first, size // 2, 0) for relative in (0, 1, 3, 2) for first in (0, size // 2)]

    def tip(x):
        return x[0, :16, :128]

    def both_ways(up, down):
        return lax.ppermute(up, "rep", up_pairs), lax.ppermute(down, "rep", down_pairs)

    def half_plan(size):
        return [(relative * size + first, size // 2, 0) for relative in (0, 1, 3, 2) for first in (0, size // 2)]

    def far_plan(size):
        half = size // 2
        return [(2 * size, half, 0), (2 * size + half, half, 0)]

    def exchange(x):
        return lax.all_to_all(x, "fsdp", split_axis=0, concat_axis=0, tiled=True)

    def applied(held, base, depth, order_after):
        strip = pl.BlockSpec((columns, 1, band, width), lambda s: (0, s, 0, 0))
        matrix = pl.BlockSpec((1, order, order), lambda s: (s + base, 0, 0))
        return call(
            apply_kernel,
            (piece(columns, depth),),
            (held, precond_left, precond_right),
            (strip, matrix, matrix),
            (strip,),
            after=order_after,
            grid=(depth,),
            limit=24,
        )

    def placed(table, plan, sources, out, after=()):
        operands = (table, *sources) if out is None else (table, *sources, out)
        specs = [SMEM] + [VMEM] * len(sources) + ([] if out is None else [HBM])

        def kernel(*refs):
            place_kernel(plan, last, *refs[: 1 + len(plan)], *refs[-2:])

        return call(
            kernel,
            (piece(blocks),),
            operands,
            specs,
            (HBM,),
            [pltpu.SemaphoreType.DMA],
            after,
            nbytes(2 * sum(p[1] for p in plan)),
            aliases=None if out is None else {1 + len(sources): 0},
        )

    order = factor_left.shape[1]
    depth_rest = slots - 1
    half_first, half_rest = size_first // 2, size_rest // 2
    low_first, high_first, mark = call(
        functools.partial(first_kernel, size_first),
        (piece(half_first), piece(half_first)),
        (table_first, rows),
        (SMEM, HBM),
        (VMEM, VMEM),
        [pltpu.SemaphoreType.DMA((2,))],
        moved=nbytes(2 * size_first),
        limit=60,
    )
    got_low_first, got_high_first = both_ways(low_first, high_first)

    def lay(table, size, parts, marks):
        def kernel(table, rows, *outs):
            lay_kernel([(p[0] * size + p[1], out) for p, out in zip(parts, outs)], table, rows)

        return call(
            kernel,
            tuple(piece(p[-1]) for p in parts),
            (table, rows),
            (SMEM, VMEM),
            (VMEM,) * len(parts),
            after=marks,
            moved=nbytes(2 * sum(p[-1] for p in parts)),
        )

    plain_up, plain_down, near_low, near_high, mine_first, mark = lay(
        table_first,
        size_first,
        [
            (1, half_first, half_first),
            (3, 0, half_first),
            (1, 0, half_first),
            (3, half_first, half_first),
            (0, 0, size_first),
        ],
        (mark,),
    )
    up_high, down_low = both_ways(plain_up, plain_down)
    low, high, mark = call(
        second_kernel,
        (piece(half_first), piece(half_first)),
        (got_low_first, got_high_first, near_low, near_high),
        (VMEM,) * 4,
        (VMEM, VMEM),
        moved=nbytes(3 * size_first),
    )
    up_low, down_high = both_ways(low, high)
    low_rest, high_rest, up_rest, down_rest, mine_rest, mark = lay(
        table_rest,
        size_rest,
        [
            (2, 0, half_rest),
            (2, half_rest, half_rest),
            (1, 0, size_rest),
            (3, 0, size_rest),
            (0, 0, size_rest),
        ],
        (mark,),
    )
    got_low_rest, got_high_rest = both_ways(low_rest, high_rest)
    sent_first, mark = call(
        functools.partial(third_first_kernel, size_first, last),
        (piece(columns, 1),),
        (table_first, mine_first, up_low, up_high, down_low, down_high),
        (SMEM,) + (VMEM,) * 5,
        (VMEM,),
        after=(mark,),
        moved=nbytes(4 * size_first),
    )
    held_first = exchange(sent_first)
    up, down, mark = call(
        second_whole_kernel,
        (piece(size_rest), piece(size_rest)),
        (got_low_rest, got_high_rest, up_rest, down_rest),
        (VMEM,) * 4,
        (VMEM, VMEM),
        after=(mark,),
        moved=nbytes(3 * size_rest),
        aliases={2: 0, 3: 1},
    )
    from_up, from_down = both_ways(up, down)
    shaped_first, mark = applied(held_first, 0, 1, ())
    sent_rest, mark = call(
        functools.partial(third_kernel, size_rest, 1, last),
        (piece(columns, slots),),
        (table_rest, place, mine_rest, from_up, from_down, shaped_first),
        (SMEM, SMEM, VMEM, VMEM, VMEM, VMEM),
        (VMEM,),
        moved=nbytes(5 * size_rest),
    )
    mixed = exchange(sent_rest)
    own_low, own_high, mark = call(
        functools.partial(take_kernel, slots - 1),
        (piece(half_first), piece(half_first)),
        (mixed,),
        (VMEM,),
        (VMEM, VMEM),
        moved=nbytes(2 * size_first),
    )
    below_low, above_high = both_ways(own_low, own_high)
    below_high, above_low = both_ways(own_high, own_low)
    far_low, far_high = both_ways(below_low, above_high)
    shaped_rest, mark = applied(mixed, 1, depth_rest, (mark,))
    back_rest = exchange(shaped_rest)
    direction, mark_placed = placed(
        table_first,
        half_plan(size_first),
        [own_low, own_high, above_low, above_high, below_low, below_high, far_low, far_high],
        None,
    )

    low, high, mark = call(
        functools.partial(pack_kernel, half_rest, 1, last),
        (piece(half_rest), piece(half_rest)),
        (table_rest, place, back_rest),
        (SMEM, SMEM, VMEM),
        (VMEM, VMEM),
        after=(mark_placed,),
        moved=nbytes(2 * size_rest),
    )
    below_low, above_high = both_ways(low, high)
    below_high, above_low = both_ways(high, low)
    far_low, far_high = both_ways(below_low, above_high)

    matrix = pl.BlockSpec((1, order, order), lambda s: (s, 0, 0))
    new_left, new_right, mark_gram = call(
        gram_kernel,
        (
            jax.ShapeDtypeStruct(factor_left.shape, F32),
            jax.ShapeDtypeStruct(factor_right.shape, F32),
        ),
        (held_first, mixed, factor_left, factor_right),
        (
            pl.BlockSpec((columns, 1, band, width), lambda s: (0, 0, 0, 0)),
            pl.BlockSpec((columns, 1, band, width), lambda s: (0, jnp.maximum(s - 1, 0), 0, 0)),
            matrix,
            matrix,
        ),
        (matrix, matrix),
        after=(mark,),
        moved=slots * 18 * order * order,
        flops=slots * 4 * order**3,
        grid=(slots,),
        limit=32,
    )

    plan = half_plan(size_rest)
    direction, _ = placed(
        table_rest, plan[:6], [low, high, above_low, above_high, below_low, below_high], direction
    )
    direction, _ = placed(table_rest, plan[6:], [far_low, far_high], direction)
    return (new_left, new_right, direction)


def solution(mesh):
    placed = (
        P("rep", None, "fsdp", None),
        P(),
        P(("rep", "fsdp"), None, None),
        P(("rep", "fsdp"), None, None),
        P(("rep", "fsdp"), None, None),
        P(("rep", "fsdp"), None, None),
    )
    return jax.shard_map(
        local,
        mesh=mesh,
        in_specs=placed,
        out_specs=(
            P(("rep", "fsdp"), None, None),
            P(("rep", "fsdp"), None, None),
            P(None, "fsdp", None),
        ),
        check_vma=False,
    )
```

```python
import functools

import jax
import jax.numpy as jnp
from jax import lax
from jax.experimental import pallas as pl
from jax.experimental.pallas import tpu as pltpu
from jax.sharding import PartitionSpec as P

epsilon = 1e-06
decay_rate = 0.9

ANY = pl.BlockSpec(memory_space=pl.ANY)
HBM = pl.BlockSpec(memory_space=pltpu.HBM)
SMEM = pl.BlockSpec(memory_space=pltpu.SMEM)
VMEM = pl.BlockSpec(memory_space=pltpu.VMEM)
F32 = jnp.float32
MIB = 1024 * 1024


def cost(nbytes, flops=0):
    return pl.CostEstimate(flops=flops, bytes_accessed=nbytes, transcendentals=0)


def batched(count, read, write, batch=4):
    def some(i, _):
        pieces = [read(batch * i + lane) for lane in range(batch)]
        for lane in range(batch):
            write(batch * i + lane, pieces[lane])
        return 0

    lax.fori_loop(0, count // batch, some, 0)


def put(out, *where):
    def write(j, piece):
        out[(j, *where)] = piece.astype(out.dtype)

    return write


def lay_kernel(plan, table, rows, zeros):
    last = rows.shape[0] - 1
    for start, out in plan:

        def read(j, start=start):
            block = table[start + j]
            piece = rows[jnp.minimum(block, last)]
            return jnp.where(block <= last, piece, jnp.zeros_like(piece)) if zeros else piece

        batched(out.shape[0], read, put(out))


def second_kernel(got_low, got_high, low_rows, high_rows, low, high):
    for got, own, out in ((got_low, low_rows, low), (got_high, high_rows, high)):
        batched(
            out.shape[0],
            lambda j, got=got, own=own: own[j].astype(F32) + got[j].astype(F32),
            put(out),
        )


def second_whole_kernel(got_low, got_high, up_rows, down_rows, up, down):
    half = got_low.shape[0]

    def write_up(j, piece):
        up[half + j] = piece

    def write_down(j, piece):
        down[half + j] = piece.astype(down.dtype)

    batched(half, lambda j: up_rows[j].astype(F32) + got_low[j].astype(F32), put(up))
    batched(half, lambda j: up_rows[half + j], write_up)
    batched(half, lambda j: down_rows[j], put(down))
    batched(half, lambda j: down_rows[half + j].astype(F32) + got_high[j].astype(F32), write_down)


def third_first_kernel(own, up_low, up_high, down_low, down_high, out):
    half = up_low.shape[0]
    for first, from_up, from_down in ((0, up_low, down_low), (half, up_high, down_high)):

        def read(k, first=first, from_up=from_up, from_down=from_down):
            return own[first + k].astype(F32) + from_up[k].astype(F32) + from_down[k].astype(F32)

        def write(k, piece, first=first):
            out[first + k, 0] = piece.astype(out.dtype)

        batched(half, read, write)


def third_kernel(size, base, last, table, place, own, from_up, from_down, out):
    for part in range(out.shape[1]):
        batched(out.shape[0], lambda j: jnp.zeros(out.shape[2:], F32), put(out, part))
    count = lax.fori_loop(0, size, lambda j, n: n + jnp.where(table[j] <= last, 1, 0), 0, unroll=8)

    def some(i, _):
        entries = [jnp.minimum(4 * i + lane, count - 1) for lane in range(4)]
        totals = [own[j].astype(F32) + from_up[j].astype(F32) + from_down[j].astype(F32) for j in entries]
        for j, total in zip(entries, totals):
            where = place[table[j]]
            out[where & 31, (where >> 5) - base] = total.astype(out.dtype)
        return 0

    lax.fori_loop(0, (count + 3) // 4, some, 0)


def pack_kernel(half, base, last, table, place, returned, low, high):
    for first, out in ((0, low), (half, high)):

        def read(j, first=first):
            where = place[jnp.minimum(table[first + j], last)]
            return returned[where & 31, jnp.maximum((where >> 5) - base, 0)]

        batched(half, read, put(out))


def take_kernel(part, mixed, low, high):
    half = low.shape[0]
    batched(half, lambda j: mixed[j, part], put(low))
    batched(half, lambda j: mixed[half + j, part], put(high))


def place_kernel(plan, last, table, *refs):
    sources, out, sem = refs[: len(plan)], refs[-2], refs[-1]

    def each(act):
        for source, (start, count, shift) in zip(sources, plan):

            def one(j, _, source=source, start=start, shift=shift):
                block = table[start + j]

                @pl.when(block <= last)
                def _():
                    act(pltpu.make_async_copy(source.at[shift + j], out.at[block], sem))

                return 0

            lax.fori_loop(0, count, one, 0)

    each(lambda copy: copy.start())
    each(lambda copy: copy.wait())


def apply_kernel(held, left, right, shaped):
    order = left.shape[-1]
    block = held[...].reshape(order, order)
    applied = jnp.dot(left[0], block, preferred_element_type=F32).astype(jnp.bfloat16)
    product = jnp.dot(applied, right[0], preferred_element_type=F32)
    wide = block.astype(F32)
    count = order * order
    held_power = jnp.sum(wide * wide) / count
    power = jnp.sum(product * product) / count
    scale = jnp.sqrt((held_power + epsilon) / (power + epsilon))
    shaped[...] = (product * scale).astype(jnp.bfloat16).reshape(shaped.shape)


def gram_kernel(held_first, held_rest, left, right, new_left, new_right):
    order = left.shape[-1]
    block = jnp.where(pl.program_id(0) == 0, held_first[...], held_rest[...]).reshape(order, order)
    weight = (1.0 - decay_rate) / order
    left_gram = lax.dot_general(block, block, (((1,), (1,)), ((), ())), preferred_element_type=F32)
    right_gram = lax.dot_general(block, block, (((0,), (0,)), ((), ())), preferred_element_type=F32)
    new_left[0] = decay_rate * left[0] + weight * left_gram
    new_right[0] = decay_rate * right[0] + weight * right_gram


def step(size_rest, grads, owner, factor_left, factor_right, precond_left, precond_right):
    rows = grads[0]
    blocks, band, width = rows.shape
    columns = lax.axis_size("fsdp")
    replicas = lax.axis_size("rep")
    my_rep = lax.axis_index("rep")
    slots = factor_left.shape[0]
    last = blocks - 1
    up_pairs = [(i, (i + 1) % replicas) for i in range(replicas)]
    down_pairs = [(i, (i - 1) % replicas) for i in range(replicas)]
    far_pairs = [(i, (i + 2) % replicas) for i in range(replicas)]

    position = jnp.arange(blocks, dtype=jnp.int32)
    earlier = position[None, :] < position[:, None]
    same_owner = (owner[:, None] == owner[None, :]) & earlier
    col_rank = jnp.sum(same_owner.astype(jnp.int32), axis=1)
    rep_of = col_rank % replicas
    local_slot = col_rank // replicas
    relative = (rep_of - my_rep) % replicas
    place = local_slot * columns + owner

    def listed(key, size):
        hits = key[None, :] == jnp.arange(size, dtype=jnp.int32)[:, None]
        return jnp.min(jnp.where(hits, position[None, :], blocks), axis=1)

    size_first = columns
    by_column = relative * columns + owner
    table_first = listed(jnp.where(local_slot == 0, by_column, -1), replicas * columns)

    def packed(member, size):
        same_list = (rep_of[:, None] == rep_of[None, :]) & member[None, :] & earlier
        in_list = jnp.sum(same_list.astype(jnp.int32), axis=1)
        return listed(jnp.where(member, relative * size + in_list, -1), replicas * size)

    table_rest = packed(local_slot > 0, size_rest)

    def piece(*count):
        return jax.ShapeDtypeStruct((*count, band, width), jnp.bfloat16)

    def nbytes(count):
        return count * band * width * 2

    token = jax.ShapeDtypeStruct((8, 128), F32)

    def call(kernel, results, operands, specs, out_specs, scratch=(), after=(), moved=0, flops=0, grid=None, aliases=None, limit=16):
        count, late = len(operands), len(after)
        n_out = len(results)
        small = pl.BlockSpec((8, 128), lambda *_: (0, 0)) if grid else VMEM

        def body(*refs):
            outs = refs[count + late : count + late + n_out]
            mark = refs[count + late + n_out]
            mark[...] = jnp.zeros_like(mark)
            kernel(*refs[:count], *outs, *refs[count + late + n_out + 1 :])

        extra = {} if grid is None else {"grid": grid}
        return pl.pallas_call(
            body,
            out_shape=(*results, token),
            in_specs=list(specs) + [ANY] * late,
            out_specs=(*out_specs, small),
            scratch_shapes=list(scratch),
            input_output_aliases=aliases or {},
            compiler_params=pltpu.CompilerParams(vmem_limit_bytes=limit * MIB),
            cost_estimate=pl.CostEstimate(flops=flops, bytes_accessed=moved, transcendentals=0),
            **extra,
        )(*operands, *after)

    def tip(x):
        return x[0, :16, :128]

    def gate(values, *marks):
        shapes = tuple(jax.ShapeDtypeStruct(v.shape, v.dtype) for v in values)
        return pl.pallas_call(
            lambda *refs: None,
            out_shape=shapes,
            in_specs=[ANY] * (len(values) + len(marks)),
            out_specs=(ANY,) * len(values),
            input_output_aliases={i: i for i in range(len(values))},
        )(*values, *marks)

    def both_ways(up, down):
        return lax.ppermute(up, "rep", up_pairs), lax.ppermute(down, "rep", down_pairs)

    def half_plan(size):
        return [(relative * size + first, size // 2, 0) for relative in (0, 1, 3, 2) for first in (0, size // 2)]

    def tip(x):
        return x[0, :16, :128]

    def both_ways(up, down):
        return lax.ppermute(up, "rep", up_pairs), lax.ppermute(down, "rep", down_pairs)

    def half_plan(size):
        return [(relative * size + first, size // 2, 0) for relative in (0, 1, 3, 2) for first in (0, size // 2)]

    def far_plan(size):
        half = size // 2
        return [(2 * size, half, 0), (2 * size + half, half, 0)]

    def exchange(x):
        return lax.all_to_all(x, "fsdp", split_axis=0, concat_axis=0, tiled=True)

    def applied(held, base, depth, order_after, moved=0):
        strip = pl.BlockSpec((columns, 1, band, width), lambda s: (0, s, 0, 0))
        matrix = pl.BlockSpec((1, order, order), lambda s: (s + base, 0, 0))
        return call(
            apply_kernel,
            (piece(columns, depth),),
            (held, precond_left, precond_right),
            (strip, matrix, matrix),
            (strip,),
            after=order_after,
            moved=moved,
            grid=(depth,),
            limit=16,
        )

    def placed(table, plan, sources, out, after=(), limit=16):
        operands = (table, *sources) if out is None else (table, *sources, out)
        specs = [SMEM] + [VMEM] * len(sources) + ([] if out is None else [HBM])

        def kernel(*refs):
            place_kernel(plan, last, *refs[: 1 + len(plan)], *refs[-2:])

        return call(
            kernel,
            (piece(blocks),),
            operands,
            specs,
            (HBM,),
            [pltpu.SemaphoreType.DMA],
            after,
            nbytes(2 * sum(p[1] for p in plan)),
            aliases=None if out is None else {1 + len(sources): 0},
            limit=limit,
        )

    order = factor_left.shape[1]
    depth_rest = slots - 1
    half_first, half_rest = size_first // 2, size_rest // 2
    def lay(table, size, parts, marks, zeros):
        def kernel(table, rows, *outs):
            lay_kernel([(p[0] * size + p[1], out) for p, out in zip(parts, outs)], table, rows, zeros)

        return call(
            kernel,
            tuple(piece(p[-1]) for p in parts),
            (table, rows),
            (SMEM, VMEM),
            (VMEM,) * len(parts),
            after=marks,
            moved=nbytes(2 * sum(p[-1] for p in parts)),
        )

    low_first, high_first, plain_up, plain_down, near_low, near_high, mine_first, mark = lay(
        table_first,
        size_first,
        [
            (2, 0, half_first),
            (2, half_first, half_first),
            (1, half_first, half_first),
            (3, 0, half_first),
            (1, 0, half_first),
            (3, half_first, half_first),
            (0, 0, size_first),
        ],
        (),
        True,
    )
    got_low_first, got_high_first = both_ways(low_first, high_first)
    up_high, down_low = both_ways(plain_up, plain_down)
    low, high, mark = call(
        second_kernel,
        (piece(half_first), piece(half_first)),
        (got_low_first, got_high_first, near_low, near_high),
        (VMEM,) * 4,
        (VMEM, VMEM),
        moved=nbytes(3 * size_first),
    )
    up_low, down_high = both_ways(low, high)
    low_rest, high_rest, up_rest, down_rest, mine_rest, mark = lay(
        table_rest,
        size_rest,
        [(2, 0, half_rest), (2, half_rest, half_rest), (1, 0, size_rest), (3, 0, size_rest), (0, 0, size_rest)],
        (mark,),
        False,
    )
    sent_first, mark = call(
        third_first_kernel,
        (piece(columns, 1),),
        (mine_first, up_low, up_high, down_low, down_high),
        (VMEM,) * 5,
        (VMEM,),
        after=(mark,),
        moved=nbytes(4 * size_first),
    )
    low_rest, high_rest = gate((low_rest, high_rest), mark)
    got_low_rest, got_high_rest = both_ways(low_rest, high_rest)
    held_first = exchange(sent_first)
    up, down, mark = call(
        second_whole_kernel,
        (piece(size_rest), piece(size_rest)),
        (got_low_rest, got_high_rest, up_rest, down_rest),
        (VMEM,) * 4,
        (VMEM, VMEM),
        after=(mark,),
        moved=nbytes(3 * size_rest),
    )
    from_up, from_down = both_ways(up, down)
    shaped_first, mark = applied(held_first, 0, 1, (mark,))
    back_first = exchange(shaped_first)
    own_low, own_high, mark = call(
        functools.partial(take_kernel, 0),
        (piece(half_first), piece(half_first)),
        (back_first,),
        (VMEM,),
        (VMEM, VMEM),
        moved=nbytes(2 * size_first),
    )
    sent_rest, _ = call(
        functools.partial(third_kernel, size_rest, 1, last),
        (piece(columns, depth_rest),),
        (table_rest, place, mine_rest, from_up, from_down),
        (SMEM, SMEM, VMEM, VMEM, VMEM),
        (VMEM,),
        moved=nbytes(5 * size_rest),
    )
    [sent_rest] = gate((sent_rest,), mark)
    held_rest = exchange(sent_rest)
    below_low, above_high = both_ways(own_low, own_high)
    below_high, above_low = both_ways(own_high, own_low)
    far_low, far_high = both_ways(below_low, above_high)
    far_first = [far_low, far_high]
    shaped_rest, mark = applied(held_rest, 1, depth_rest, (tip(below_low), tip(above_high)))
    back_rest = exchange(shaped_rest)
    plan_first = half_plan(size_first)
    direction, mark_placed = placed(
        table_first,
        plan_first[:6],
        [own_low, own_high, above_low, above_high, below_low, below_high],
        None,
    )
    low, high, mark = call(
        functools.partial(pack_kernel, half_rest, 1, last),
        (piece(half_rest), piece(half_rest)),
        (table_rest, place, back_rest),
        (SMEM, SMEM, VMEM),
        (VMEM, VMEM),
        after=(mark_placed, tip(far_first[0]), tip(far_first[1])),
        moved=nbytes(2 * size_rest),
    )
    below_low, above_high = both_ways(low, high)
    below_high, above_low = both_ways(high, low)
    far_low, far_high = both_ways(below_low, above_high)

    matrix = pl.BlockSpec((1, order, order), lambda s: (s, 0, 0))
    new_left, new_right, _ = call(
        gram_kernel,
        (
            jax.ShapeDtypeStruct(factor_left.shape, F32),
            jax.ShapeDtypeStruct(factor_right.shape, F32),
        ),
        (held_first, held_rest, factor_left, factor_right),
        (
            pl.BlockSpec((columns, 1, band, width), lambda s: (0, 0, 0, 0)),
            pl.BlockSpec((columns, 1, band, width), lambda s: (0, jnp.maximum(s - 1, 0), 0, 0)),
            matrix,
            matrix,
        ),
        (matrix, matrix),
        after=(mark,),
        moved=slots * 18 * order * order,
        flops=slots * 4 * order**3,
        grid=(slots,),
        limit=24,
    )

    direction, _ = placed(table_first, plan_first[6:], far_first, direction)
    plan = half_plan(size_rest)
    direction, _ = placed(
        table_rest, plan[:6], [low, high, above_low, above_high, below_low, below_high], direction, (), 59
    )
    direction, _ = placed(table_rest, plan[6:], [far_low, far_high], direction, (), 59)
    return (new_left, new_right, direction)


def local(grads, owner, *others):
    columns = jnp.arange(lax.axis_size("fsdp"), dtype=jnp.int32)
    counts = jnp.sum((owner[None, :] == columns[:, None]).astype(jnp.int32), axis=1)
    longest = jnp.sum((counts > 4).astype(jnp.int32) + (counts > 8).astype(jnp.int32))
    return lax.cond(
        longest <= 48,
        functools.partial(step, 48),
        functools.partial(step, 56),
        grads,
        owner,
        *others,
    )


def solution(mesh):
    placed = (
        P("rep", None, "fsdp", None),
        P(),
        P(("rep", "fsdp"), None, None),
        P(("rep", "fsdp"), None, None),
        P(("rep", "fsdp"), None, None),
        P(("rep", "fsdp"), None, None),
    )
    return jax.shard_map(
        local,
        mesh=mesh,
        in_specs=placed,
        out_specs=(
            P(("rep", "fsdp"), None, None),
            P(("rep", "fsdp"), None, None),
            P(None, "fsdp", None),
        ),
        check_vma=False,
    )
```

```python
import functools

import jax
import jax.numpy as jnp
from jax import lax
from jax.experimental import pallas as pl
from jax.experimental.pallas import tpu as pltpu
from jax.sharding import PartitionSpec as P

epsilon = 1e-06
decay_rate = 0.9

ANY = pl.BlockSpec(memory_space=pl.ANY)
HBM = pl.BlockSpec(memory_space=pltpu.HBM)
SMEM = pl.BlockSpec(memory_space=pltpu.SMEM)
VMEM = pl.BlockSpec(memory_space=pltpu.VMEM)
F32 = jnp.float32
MIB = 1024 * 1024


def cost(nbytes, flops=0):
    return pl.CostEstimate(flops=flops, bytes_accessed=nbytes, transcendentals=0)


def batched(count, read, write, batch=4):
    def some(i, _):
        pieces = [read(batch * i + lane) for lane in range(batch)]
        for lane in range(batch):
            write(batch * i + lane, pieces[lane])
        return 0

    lax.fori_loop(0, count // batch, some, 0)


def put(out, *where):
    def write(j, piece):
        out[(j, *where)] = piece.astype(out.dtype)

    return write


def lay_kernel(plan, table, rows, zeros):
    last = rows.shape[0] - 1
    for start, out in plan:

        def read(j, start=start):
            block = table[start + j]
            piece = rows[jnp.minimum(block, last)]
            return jnp.where(block <= last, piece, jnp.zeros_like(piece)) if zeros else piece

        batched(out.shape[0], read, put(out))


def second_kernel(got_low, got_high, low_rows, high_rows, low, high):
    for got, own, out in ((got_low, low_rows, low), (got_high, high_rows, high)):
        batched(
            out.shape[0],
            lambda j, got=got, own=own: own[j].astype(F32) + got[j].astype(F32),
            put(out),
        )


def second_whole_kernel(got_low, got_high, up_rows, down_rows, up, down):
    half = got_low.shape[0]

    def write_up(j, piece):
        up[half + j] = piece

    def write_down(j, piece):
        down[half + j] = piece.astype(down.dtype)

    batched(half, lambda j: up_rows[j].astype(F32) + got_low[j].astype(F32), put(up))
    batched(half, lambda j: up_rows[half + j], write_up)
    batched(half, lambda j: down_rows[j], put(down))
    batched(half, lambda j: down_rows[half + j].astype(F32) + got_high[j].astype(F32), write_down)


def third_first_kernel(own, up_low, up_high, down_low, down_high, out):
    half = up_low.shape[0]
    for first, from_up, from_down in ((0, up_low, down_low), (half, up_high, down_high)):

        def read(k, first=first, from_up=from_up, from_down=from_down):
            return own[first + k].astype(F32) + from_up[k].astype(F32) + from_down[k].astype(F32)

        def write(k, piece, first=first):
            out[first + k, 0] = piece.astype(out.dtype)

        batched(half, read, write)


def third_kernel(size, base, last, table, place, own, from_up, from_down, out):
    for part in range(out.shape[1]):
        batched(out.shape[0], lambda j: jnp.zeros(out.shape[2:], F32), put(out, part))
    count = lax.fori_loop(0, size, lambda j, n: n + jnp.where(table[j] <= last, 1, 0), 0, unroll=8)

    def some(i, _):
        entries = [jnp.minimum(4 * i + lane, count - 1) for lane in range(4)]
        totals = [own[j].astype(F32) + from_up[j].astype(F32) + from_down[j].astype(F32) for j in entries]
        for j, total in zip(entries, totals):
            where = place[table[j]]
            out[where & 31, (where >> 5) - base] = total.astype(out.dtype)
        return 0

    lax.fori_loop(0, (count + 3) // 4, some, 0)


def pack_kernel(half, base, last, table, place, returned, low, high):
    for first, out in ((0, low), (half, high)):

        def read(j, first=first):
            where = place[jnp.minimum(table[first + j], last)]
            return returned[where & 31, jnp.maximum((where >> 5) - base, 0)]

        batched(half, read, put(out))


def take_kernel(part, mixed, low, high):
    half = low.shape[0]
    batched(half, lambda j: mixed[j, part], put(low))
    batched(half, lambda j: mixed[half + j, part], put(high))


def place_kernel(plan, last, table, *refs):
    sources, out, sem = refs[: len(plan)], refs[-2], refs[-1]

    def each(act):
        for source, (start, count, shift) in zip(sources, plan):

            def one(j, _, source=source, start=start, shift=shift):
                block = table[start + j]

                @pl.when(block <= last)
                def _():
                    act(pltpu.make_async_copy(source.at[shift + j], out.at[block], sem))

                return 0

            lax.fori_loop(0, count, one, 0)

    each(lambda copy: copy.start())
    each(lambda copy: copy.wait())


def apply_kernel(held, left, right, shaped):
    order = left.shape[-1]
    block = held[...].reshape(order, order)
    applied = jnp.dot(left[0], block, preferred_element_type=F32).astype(jnp.bfloat16)
    product = jnp.dot(applied, right[0], preferred_element_type=F32)
    wide = block.astype(F32)
    count = order * order
    held_power = jnp.sum(wide * wide) / count
    power = jnp.sum(product * product) / count
    scale = jnp.sqrt((held_power + epsilon) / (power + epsilon))
    shaped[...] = (product * scale).astype(jnp.bfloat16).reshape(shaped.shape)


def gram_kernel(held_first, held_rest, left, right, new_left, new_right):
    order = left.shape[-1]
    block = jnp.where(pl.program_id(0) == 0, held_first[...], held_rest[...]).reshape(order, order)
    weight = (1.0 - decay_rate) / order
    left_gram = lax.dot_general(block, block, (((1,), (1,)), ((), ())), preferred_element_type=F32)
    right_gram = lax.dot_general(block, block, (((0,), (0,)), ((), ())), preferred_element_type=F32)
    new_left[0] = decay_rate * left[0] + weight * left_gram
    new_right[0] = decay_rate * right[0] + weight * right_gram


def step(size_rest, grads, owner, factor_left, factor_right, precond_left, precond_right):
    rows = grads[0]
    blocks, band, width = rows.shape
    columns = lax.axis_size("fsdp")
    replicas = lax.axis_size("rep")
    my_rep = lax.axis_index("rep")
    slots = factor_left.shape[0]
    last = blocks - 1
    up_pairs = [(i, (i + 1) % replicas) for i in range(replicas)]
    down_pairs = [(i, (i - 1) % replicas) for i in range(replicas)]
    far_pairs = [(i, (i + 2) % replicas) for i in range(replicas)]

    position = jnp.arange(blocks, dtype=jnp.int32)
    earlier = position[None, :] < position[:, None]
    same_owner = (owner[:, None] == owner[None, :]) & earlier
    col_rank = jnp.sum(same_owner.astype(jnp.int32), axis=1)
    rep_of = col_rank % replicas
    local_slot = col_rank // replicas
    relative = (rep_of - my_rep) % replicas
    place = local_slot * columns + owner

    def listed(key, size):
        hits = key[None, :] == jnp.arange(size, dtype=jnp.int32)[:, None]
        return jnp.min(jnp.where(hits, position[None, :], blocks), axis=1)

    size_first = columns
    by_column = relative * columns + owner
    table_first = listed(jnp.where(local_slot == 0, by_column, -1), replicas * columns)

    def packed(member, size):
        same_list = (rep_of[:, None] == rep_of[None, :]) & member[None, :] & earlier
        in_list = jnp.sum(same_list.astype(jnp.int32), axis=1)
        return listed(jnp.where(member, relative * size + in_list, -1), replicas * size)

    table_rest = packed(local_slot > 0, size_rest)

    def piece(*count):
        return jax.ShapeDtypeStruct((*count, band, width), jnp.bfloat16)

    def nbytes(count):
        return count * band * width * 2

    token = jax.ShapeDtypeStruct((8, 128), F32)

    def call(kernel, results, operands, specs, out_specs, scratch=(), after=(), moved=0, flops=0, grid=None, aliases=None, limit=16):
        count, late = len(operands), len(after)
        n_out = len(results)
        small = pl.BlockSpec((8, 128), lambda *_: (0, 0)) if grid else VMEM

        def body(*refs):
            outs = refs[count + late : count + late + n_out]
            mark = refs[count + late + n_out]
            mark[...] = jnp.zeros_like(mark)
            kernel(*refs[:count], *outs, *refs[count + late + n_out + 1 :])

        extra = {} if grid is None else {"grid": grid}
        return pl.pallas_call(
            body,
            out_shape=(*results, token),
            in_specs=list(specs) + [ANY] * late,
            out_specs=(*out_specs, small),
            scratch_shapes=list(scratch),
            input_output_aliases=aliases or {},
            compiler_params=pltpu.CompilerParams(vmem_limit_bytes=limit * MIB),
            cost_estimate=pl.CostEstimate(flops=flops, bytes_accessed=moved, transcendentals=0),
            **extra,
        )(*operands, *after)

    def tip(x):
        return x[0, :16, :128]

    def gate(values, *marks):
        shapes = tuple(jax.ShapeDtypeStruct(v.shape, v.dtype) for v in values)
        return pl.pallas_call(
            lambda *refs: None,
            out_shape=shapes,
            in_specs=[ANY] * (len(values) + len(marks)),
            out_specs=(ANY,) * len(values),
            input_output_aliases={i: i for i in range(len(values))},
        )(*values, *marks)

    def both_ways(up, down):
        return lax.ppermute(up, "rep", up_pairs), lax.ppermute(down, "rep", down_pairs)

    def half_plan(size):
        return [(relative * size + first, size // 2, 0) for relative in (0, 1, 3, 2) for first in (0, size // 2)]

    def tip(x):
        return x[0, :16, :128]

    def both_ways(up, down):
        return lax.ppermute(up, "rep", up_pairs), lax.ppermute(down, "rep", down_pairs)

    def half_plan(size):
        return [(relative * size + first, size // 2, 0) for relative in (0, 1, 3, 2) for first in (0, size // 2)]

    def far_plan(size):
        half = size // 2
        return [(2 * size, half, 0), (2 * size + half, half, 0)]

    def exchange(x):
        return lax.all_to_all(x, "fsdp", split_axis=0, concat_axis=0, tiled=True)

    def applied(held, base, depth, order_after, moved=0):
        strip = pl.BlockSpec((columns, 1, band, width), lambda s: (0, s, 0, 0))
        matrix = pl.BlockSpec((1, order, order), lambda s: (s + base, 0, 0))
        return call(
            apply_kernel,
            (piece(columns, depth),),
            (held, precond_left, precond_right),
            (strip, matrix, matrix),
            (strip,),
            after=order_after,
            moved=moved,
            grid=(depth,),
            limit=16,
        )

    def placed(table, plan, sources, out, after=(), limit=16):
        operands = (table, *sources) if out is None else (table, *sources, out)
        specs = [SMEM] + [VMEM] * len(sources) + ([] if out is None else [HBM])

        def kernel(*refs):
            place_kernel(plan, last, *refs[: 1 + len(plan)], *refs[-2:])

        return call(
            kernel,
            (piece(blocks),),
            operands,
            specs,
            (HBM,),
            [pltpu.SemaphoreType.DMA],
            after,
            nbytes(2 * sum(p[1] for p in plan)),
            aliases=None if out is None else {1 + len(sources): 0},
            limit=limit,
        )

    order = factor_left.shape[1]
    depth_rest = slots - 1
    half_first, half_rest = size_first // 2, size_rest // 2
    def lay(table, size, parts, marks, zeros):
        def kernel(table, rows, *outs):
            lay_kernel([(p[0] * size + p[1], out) for p, out in zip(parts, outs)], table, rows, zeros)

        return call(
            kernel,
            tuple(piece(p[-1]) for p in parts),
            (table, rows),
            (SMEM, VMEM),
            (VMEM,) * len(parts),
            after=marks,
            moved=nbytes(2 * sum(p[-1] for p in parts)),
        )

    low_first, high_first, plain_up, plain_down, near_low, near_high, mine_first, mark = lay(
        table_first,
        size_first,
        [
            (2, 0, half_first),
            (2, half_first, half_first),
            (1, half_first, half_first),
            (3, 0, half_first),
            (1, 0, half_first),
            (3, half_first, half_first),
            (0, 0, size_first),
        ],
        (),
        True,
    )
    got_low_first, got_high_first = both_ways(low_first, high_first)
    up_high, down_low = both_ways(plain_up, plain_down)
    low, high, mark = call(
        second_kernel,
        (piece(half_first), piece(half_first)),
        (got_low_first, got_high_first, near_low, near_high),
        (VMEM,) * 4,
        (VMEM, VMEM),
        moved=nbytes(3 * size_first),
    )
    up_low, down_high = both_ways(low, high)
    low_rest, high_rest, up_rest, down_rest, mine_rest, mark = lay(
        table_rest,
        size_rest,
        [(2, 0, half_rest), (2, half_rest, half_rest), (1, 0, size_rest), (3, 0, size_rest), (0, 0, size_rest)],
        (mark,),
        False,
    )
    sent_first, mark = call(
        third_first_kernel,
        (piece(columns, 1),),
        (mine_first, up_low, up_high, down_low, down_high),
        (VMEM,) * 5,
        (VMEM,),
        after=(mark,),
        moved=nbytes(4 * size_first),
    )
    low_rest, high_rest = gate((low_rest, high_rest), mark)
    got_low_rest, got_high_rest = both_ways(low_rest, high_rest)
    held_first = exchange(sent_first)
    up, down, mark = call(
        second_whole_kernel,
        (piece(size_rest), piece(size_rest)),
        (got_low_rest, got_high_rest, up_rest, down_rest),
        (VMEM,) * 4,
        (VMEM, VMEM),
        after=(mark,),
        moved=nbytes(3 * size_rest),
    )
    from_up, from_down = both_ways(up, down)
    shaped_first, mark = applied(held_first, 0, 1, (mark,))
    back_first = exchange(shaped_first)
    own_low, own_high, mark = call(
        functools.partial(take_kernel, 0),
        (piece(half_first), piece(half_first)),
        (back_first,),
        (VMEM,),
        (VMEM, VMEM),
        moved=nbytes(2 * size_first),
    )
    sent_rest, _ = call(
        functools.partial(third_kernel, size_rest, 1, last),
        (piece(columns, depth_rest),),
        (table_rest, place, mine_rest, from_up, from_down),
        (SMEM, SMEM, VMEM, VMEM, VMEM),
        (VMEM,),
        moved=nbytes(5 * size_rest),
    )
    [sent_rest] = gate((sent_rest,), mark)
    held_rest = exchange(sent_rest)
    below_low, above_high = both_ways(own_low, own_high)
    below_high, above_low = both_ways(own_high, own_low)
    far_low, far_high = both_ways(below_low, above_high)
    far_first = [far_low, far_high]
    shaped_rest, mark = applied(held_rest, 1, depth_rest, (tip(below_low), tip(above_high)))
    back_rest = exchange(shaped_rest)
    plan_first = half_plan(size_first)
    direction, mark_placed = placed(
        table_first,
        plan_first[:6],
        [own_low, own_high, above_low, above_high, below_low, below_high],
        None,
    )
    low, high, mark = call(
        functools.partial(pack_kernel, half_rest, 1, last),
        (piece(half_rest), piece(half_rest)),
        (table_rest, place, back_rest),
        (SMEM, SMEM, VMEM),
        (VMEM, VMEM),
        after=(mark_placed, tip(far_first[0]), tip(far_first[1])),
        moved=nbytes(2 * size_rest),
    )
    below_low, above_high = both_ways(low, high)
    below_high, above_low = both_ways(high, low)
    matrix = pl.BlockSpec((1, order, order), lambda s: (s, 0, 0))
    new_left, new_right, mark = call(
        gram_kernel,
        (
            jax.ShapeDtypeStruct(factor_left.shape, F32),
            jax.ShapeDtypeStruct(factor_right.shape, F32),
        ),
        (held_first, held_rest, factor_left, factor_right),
        (
            pl.BlockSpec((columns, 1, band, width), lambda s: (0, 0, 0, 0)),
            pl.BlockSpec((columns, 1, band, width), lambda s: (0, jnp.maximum(s - 1, 0), 0, 0)),
            matrix,
            matrix,
        ),
        (matrix, matrix),
        after=(mark,),
        moved=slots * 18 * order * order,
        flops=slots * 4 * order**3,
        grid=(slots,),
        limit=24,
    )

    below_low, above_high = gate((below_low, above_high), mark)
    far_low, far_high = both_ways(below_low, above_high)

    direction, _ = placed(table_first, plan_first[6:], far_first, direction)
    plan = half_plan(size_rest)
    direction, _ = placed(
        table_rest, plan[:6], [low, high, above_low, above_high, below_low, below_high], direction, (), 59
    )
    direction, _ = placed(table_rest, plan[6:], [far_low, far_high], direction, (), 59)
    return (new_left, new_right, direction)


def local(grads, owner, *others):
    columns = jnp.arange(lax.axis_size("fsdp"), dtype=jnp.int32)
    counts = jnp.sum((owner[None, :] == columns[:, None]).astype(jnp.int32), axis=1)
    longest = jnp.sum((counts > 4).astype(jnp.int32) + (counts > 8).astype(jnp.int32))
    return lax.cond(
        longest <= 48,
        functools.partial(step, 48),
        functools.partial(step, 56),
        grads,
        owner,
        *others,
    )


def solution(mesh):
    placed = (
        P("rep", None, "fsdp", None),
        P(),
        P(("rep", "fsdp"), None, None),
        P(("rep", "fsdp"), None, None),
        P(("rep", "fsdp"), None, None),
        P(("rep", "fsdp"), None, None),
    )
    return jax.shard_map(
        local,
        mesh=mesh,
        in_specs=placed,
        out_specs=(
            P(("rep", "fsdp"), None, None),
            P(("rep", "fsdp"), None, None),
            P(None, "fsdp", None),
        ),
        check_vma=False,
    )
```

```python
import functools

import jax
import jax.numpy as jnp
from jax import lax
from jax.experimental import pallas as pl
from jax.experimental.pallas import tpu as pltpu
from jax.sharding import PartitionSpec as P

epsilon = 1e-06
decay_rate = 0.9

ANY = pl.BlockSpec(memory_space=pl.ANY)
HBM = pl.BlockSpec(memory_space=pltpu.HBM)
SMEM = pl.BlockSpec(memory_space=pltpu.SMEM)
VMEM = pl.BlockSpec(memory_space=pltpu.VMEM)
F32 = jnp.float32
MIB = 1024 * 1024


def cost(nbytes, flops=0):
    return pl.CostEstimate(flops=flops, bytes_accessed=nbytes, transcendentals=0)


def batched(count, read, write, batch=4):
    def some(i, _):
        pieces = [read(batch * i + lane) for lane in range(batch)]
        for lane in range(batch):
            write(batch * i + lane, pieces[lane])
        return 0

    lax.fori_loop(0, count // batch, some, 0)


def put(out, *where):
    def write(j, piece):
        out[(j, *where)] = piece.astype(out.dtype)

    return write


def lay_kernel(plan, table, rows, zeros):
    last = rows.shape[0] - 1
    for start, out in plan:

        def read(j, start=start):
            block = table[start + j]
            piece = rows[jnp.minimum(block, last)]
            return jnp.where(block <= last, piece, jnp.zeros_like(piece)) if zeros else piece

        batched(out.shape[0], read, put(out))


def second_kernel(got_low, got_high, low_rows, high_rows, low, high):
    for got, own, out in ((got_low, low_rows, low), (got_high, high_rows, high)):
        batched(
            out.shape[0],
            lambda j, got=got, own=own: own[j].astype(F32) + got[j].astype(F32),
            put(out),
        )


def second_whole_kernel(got_low, got_high, up_rows, down_rows, up, down):
    half = got_low.shape[0]

    def write_up(j, piece):
        up[half + j] = piece

    def write_down(j, piece):
        down[half + j] = piece.astype(down.dtype)

    batched(half, lambda j: up_rows[j].astype(F32) + got_low[j].astype(F32), put(up))
    batched(half, lambda j: up_rows[half + j], write_up)
    batched(half, lambda j: down_rows[j], put(down))
    batched(half, lambda j: down_rows[half + j].astype(F32) + got_high[j].astype(F32), write_down)


def third_first_kernel(own, up_low, up_high, down_low, down_high, out):
    half = up_low.shape[0]
    for first, from_up, from_down in ((0, up_low, down_low), (half, up_high, down_high)):

        def read(k, first=first, from_up=from_up, from_down=from_down):
            return own[first + k].astype(F32) + from_up[k].astype(F32) + from_down[k].astype(F32)

        def write(k, piece, first=first):
            out[first + k, 0] = piece.astype(out.dtype)

        batched(half, read, write)


def third_kernel(size, base, last, table, place, own, from_up, from_down, out):
    for part in range(out.shape[1]):
        batched(out.shape[0], lambda j: jnp.zeros(out.shape[2:], F32), put(out, part))
    count = lax.fori_loop(0, size, lambda j, n: n + jnp.where(table[j] <= last, 1, 0), 0, unroll=8)

    def some(i, _):
        entries = [jnp.minimum(4 * i + lane, count - 1) for lane in range(4)]
        totals = [own[j].astype(F32) + from_up[j].astype(F32) + from_down[j].astype(F32) for j in entries]
        for j, total in zip(entries, totals):
            where = place[table[j]]
            out[where & 31, (where >> 5) - base] = total.astype(out.dtype)
        return 0

    lax.fori_loop(0, (count + 3) // 4, some, 0)


def pack_kernel(half, base, last, table, place, returned, low, high):
    for first, out in ((0, low), (half, high)):

        def read(j, first=first):
            where = place[jnp.minimum(table[first + j], last)]
            return returned[where & 31, jnp.maximum((where >> 5) - base, 0)]

        batched(half, read, put(out))


def take_kernel(part, mixed, low, high):
    half = low.shape[0]
    batched(half, lambda j: mixed[j, part], put(low))
    batched(half, lambda j: mixed[half + j, part], put(high))


def place_kernel(plan, last, table, *refs):
    sources, out, sem = refs[: len(plan)], refs[-2], refs[-1]
    started = jnp.int32(0)
    for source, (start, count, shift) in zip(sources, plan):

        def one(j, n, source=source, start=start, shift=shift):
            block = table[start + j]

            @pl.when(block <= last)
            def _():
                pltpu.make_async_copy(source.at[shift + j], out.at[block], sem).start()

            return n + jnp.where(block <= last, 1, 0)

        started = lax.fori_loop(0, count, one, started, unroll=4)

    def done(_, n):
        pltpu.make_async_copy(sources[0].at[0], out.at[0], sem).wait()
        return n

    lax.fori_loop(0, started, done, 0)


def apply_kernel(held, left, right, shaped):
    order = left.shape[-1]
    block = held[...].reshape(order, order)
    applied = jnp.dot(left[0], block, preferred_element_type=F32).astype(jnp.bfloat16)
    product = jnp.dot(applied, right[0], preferred_element_type=F32)
    wide = block.astype(F32)
    count = order * order
    held_power = jnp.sum(wide * wide) / count
    power = jnp.sum(product * product) / count
    scale = jnp.sqrt((held_power + epsilon) / (power + epsilon))
    shaped[...] = (product * scale).astype(jnp.bfloat16).reshape(shaped.shape)


def gram_kernel(held_first, held_rest, left, right, new_left, new_right):
    order = left.shape[-1]
    block = jnp.where(pl.program_id(0) == 0, held_first[...], held_rest[...]).reshape(order, order)
    weight = (1.0 - decay_rate) / order
    left_gram = lax.dot_general(block, block, (((1,), (1,)), ((), ())), preferred_element_type=F32)
    right_gram = lax.dot_general(block, block, (((0,), (0,)), ((), ())), preferred_element_type=F32)
    new_left[0] = decay_rate * left[0] + weight * left_gram
    new_right[0] = decay_rate * right[0] + weight * right_gram


def step(size_rest, grads, owner, col_rank, factor_left, factor_right, precond_left, precond_right):
    rows = grads[0]
    blocks, band, width = rows.shape
    columns = lax.axis_size("fsdp")
    replicas = lax.axis_size("rep")
    my_rep = lax.axis_index("rep")
    slots = factor_left.shape[0]
    last = blocks - 1
    up_pairs = [(i, (i + 1) % replicas) for i in range(replicas)]
    down_pairs = [(i, (i - 1) % replicas) for i in range(replicas)]
    far_pairs = [(i, (i + 2) % replicas) for i in range(replicas)]

    position = jnp.arange(blocks, dtype=jnp.int32)
    earlier = position[None, :] < position[:, None]
    rep_of = col_rank % replicas
    local_slot = col_rank // replicas
    relative = (rep_of - my_rep) % replicas
    place = local_slot * columns + owner

    def listed(key, size):
        hits = key[None, :] == jnp.arange(size, dtype=jnp.int32)[:, None]
        return jnp.min(jnp.where(hits, position[None, :], blocks), axis=1)

    size_first = columns
    by_column = relative * columns + owner
    table_first = listed(jnp.where(local_slot == 0, by_column, -1), replicas * columns)

    def packed(member, size):
        same_list = (rep_of[:, None] == rep_of[None, :]) & member[None, :] & earlier
        in_list = jnp.sum(same_list.astype(jnp.int32), axis=1)
        return listed(jnp.where(member, relative * size + in_list, -1), replicas * size)

    table_rest = packed(local_slot > 0, size_rest)

    def piece(*count):
        return jax.ShapeDtypeStruct((*count, band, width), jnp.bfloat16)

    def nbytes(count):
        return count * band * width * 2

    token = jax.ShapeDtypeStruct((8, 128), F32)

    def call(kernel, results, operands, specs, out_specs, scratch=(), after=(), moved=0, flops=0, grid=None, aliases=None, limit=16):
        count, late = len(operands), len(after)
        n_out = len(results)
        small = pl.BlockSpec((8, 128), lambda *_: (0, 0)) if grid else VMEM

        def body(*refs):
            outs = refs[count + late : count + late + n_out]
            mark = refs[count + late + n_out]
            mark[...] = jnp.zeros_like(mark)
            kernel(*refs[:count], *outs, *refs[count + late + n_out + 1 :])

        extra = {} if grid is None else {"grid": grid}
        return pl.pallas_call(
            body,
            out_shape=(*results, token),
            in_specs=list(specs) + [ANY] * late,
            out_specs=(*out_specs, small),
            scratch_shapes=list(scratch),
            input_output_aliases=aliases or {},
            compiler_params=pltpu.CompilerParams(vmem_limit_bytes=limit * MIB),
            cost_estimate=pl.CostEstimate(flops=flops, bytes_accessed=moved, transcendentals=0),
            **extra,
        )(*operands, *after)

    def tip(x):
        return x[0, :16, :128]

    def gate(values, *marks):
        shapes = tuple(jax.ShapeDtypeStruct(v.shape, v.dtype) for v in values)
        return pl.pallas_call(
            lambda *refs: None,
            out_shape=shapes,
            in_specs=[ANY] * (len(values) + len(marks)),
            out_specs=(ANY,) * len(values),
            input_output_aliases={i: i for i in range(len(values))},
        )(*values, *marks)

    def both_ways(up, down):
        return lax.ppermute(up, "rep", up_pairs), lax.ppermute(down, "rep", down_pairs)

    def half_plan(size):
        return [(relative * size + first, size // 2, 0) for relative in (0, 1, 3, 2) for first in (0, size // 2)]

    def tip(x):
        return x[0, :16, :128]

    def both_ways(up, down):
        return lax.ppermute(up, "rep", up_pairs), lax.ppermute(down, "rep", down_pairs)

    def half_plan(size):
        return [(relative * size + first, size // 2, 0) for relative in (0, 1, 3, 2) for first in (0, size // 2)]

    def far_plan(size):
        half = size // 2
        return [(2 * size, half, 0), (2 * size + half, half, 0)]

    def exchange(x):
        return lax.all_to_all(x, "fsdp", split_axis=0, concat_axis=0, tiled=True)

    def applied(held, base, depth, order_after, moved=0):
        strip = pl.BlockSpec((columns, 1, band, width), lambda s: (0, s, 0, 0))
        matrix = pl.BlockSpec((1, order, order), lambda s: (s + base, 0, 0))
        return call(
            apply_kernel,
            (piece(columns, depth),),
            (held, precond_left, precond_right),
            (strip, matrix, matrix),
            (strip,),
            after=order_after,
            moved=moved,
            grid=(depth,),
            limit=16,
        )

    def placed(table, plan, sources, out, after=(), limit=16):
        operands = (table, *sources) if out is None else (table, *sources, out)
        specs = [SMEM] + [VMEM] * len(sources) + ([] if out is None else [HBM])

        def kernel(*refs):
            place_kernel(plan, last, *refs[: 1 + len(plan)], *refs[-2:])

        return call(
            kernel,
            (piece(blocks),),
            operands,
            specs,
            (HBM,),
            [pltpu.SemaphoreType.DMA],
            after,
            nbytes(2 * sum(p[1] for p in plan)),
            aliases=None if out is None else {1 + len(sources): 0},
            limit=limit,
        )

    order = factor_left.shape[1]
    depth_rest = slots - 1
    half_first, half_rest = size_first // 2, size_rest // 2
    def lay(table, size, parts, marks, zeros):
        def kernel(table, rows, *outs):
            lay_kernel([(p[0] * size + p[1], out) for p, out in zip(parts, outs)], table, rows, zeros)

        return call(
            kernel,
            tuple(piece(p[-1]) for p in parts),
            (table, rows),
            (SMEM, VMEM),
            (VMEM,) * len(parts),
            after=marks,
            moved=nbytes(2 * sum(p[-1] for p in parts)),
        )

    low_first, high_first, plain_up, plain_down, near_low, near_high, mine_first, mark = lay(
        table_first,
        size_first,
        [
            (2, 0, half_first),
            (2, half_first, half_first),
            (1, half_first, half_first),
            (3, 0, half_first),
            (1, 0, half_first),
            (3, half_first, half_first),
            (0, 0, size_first),
        ],
        (),
        True,
    )
    got_low_first, got_high_first = both_ways(low_first, high_first)
    up_high, down_low = both_ways(plain_up, plain_down)
    low, high, mark = call(
        second_kernel,
        (piece(half_first), piece(half_first)),
        (got_low_first, got_high_first, near_low, near_high),
        (VMEM,) * 4,
        (VMEM, VMEM),
        moved=nbytes(3 * size_first),
    )
    up_low, down_high = both_ways(low, high)
    low_rest, high_rest, up_rest, down_rest, mine_rest, mark = lay(
        table_rest,
        size_rest,
        [(2, 0, half_rest), (2, half_rest, half_rest), (1, 0, size_rest), (3, 0, size_rest), (0, 0, size_rest)],
        (mark,),
        False,
    )
    sent_first, mark = call(
        third_first_kernel,
        (piece(columns, 1),),
        (mine_first, up_low, up_high, down_low, down_high),
        (VMEM,) * 5,
        (VMEM,),
        after=(mark,),
        moved=nbytes(4 * size_first),
    )
    low_rest, high_rest = gate((low_rest, high_rest), mark)
    got_low_rest, got_high_rest = both_ways(low_rest, high_rest)
    held_first = exchange(sent_first)
    up, down, mark = call(
        second_whole_kernel,
        (piece(size_rest), piece(size_rest)),
        (got_low_rest, got_high_rest, up_rest, down_rest),
        (VMEM,) * 4,
        (VMEM, VMEM),
        after=(mark,),
        moved=nbytes(3 * size_rest),
    )
    from_up, from_down = both_ways(up, down)
    shaped_first, mark = applied(held_first, 0, 1, (mark,))
    back_first = exchange(shaped_first)
    own_low, own_high, mark = call(
        functools.partial(take_kernel, 0),
        (piece(half_first), piece(half_first)),
        (back_first,),
        (VMEM,),
        (VMEM, VMEM),
        moved=nbytes(2 * size_first),
    )
    sent_rest, _ = call(
        functools.partial(third_kernel, size_rest, 1, last),
        (piece(columns, depth_rest),),
        (table_rest, place, mine_rest, from_up, from_down),
        (SMEM, SMEM, VMEM, VMEM, VMEM),
        (VMEM,),
        moved=nbytes(5 * size_rest),
    )
    [sent_rest] = gate((sent_rest,), mark)
    held_rest = exchange(sent_rest)
    below_low, above_high = both_ways(own_low, own_high)
    below_high, above_low = both_ways(own_high, own_low)
    far_low, far_high = both_ways(below_low, above_high)
    far_first = [far_low, far_high]
    shaped_rest, mark = applied(held_rest, 1, depth_rest, (tip(below_low), tip(above_high)))
    back_rest = exchange(shaped_rest)
    plan_first = half_plan(size_first)
    direction, mark_placed = placed(
        table_first,
        plan_first[:6],
        [own_low, own_high, above_low, above_high, below_low, below_high],
        None,
    )
    low, high, mark = call(
        functools.partial(pack_kernel, half_rest, 1, last),
        (piece(half_rest), piece(half_rest)),
        (table_rest, place, back_rest),
        (SMEM, SMEM, VMEM),
        (VMEM, VMEM),
        after=(mark_placed, tip(far_first[0]), tip(far_first[1])),
        moved=nbytes(2 * size_rest),
    )
    below_low, above_high = both_ways(low, high)
    below_high, above_low = both_ways(high, low)
    matrix = pl.BlockSpec((1, order, order), lambda s: (s, 0, 0))
    new_left, new_right, mark = call(
        gram_kernel,
        (
            jax.ShapeDtypeStruct(factor_left.shape, F32),
            jax.ShapeDtypeStruct(factor_right.shape, F32),
        ),
        (held_first, held_rest, factor_left, factor_right),
        (
            pl.BlockSpec((columns, 1, band, width), lambda s: (0, 0, 0, 0)),
            pl.BlockSpec((columns, 1, band, width), lambda s: (0, jnp.maximum(s - 1, 0), 0, 0)),
            matrix,
            matrix,
        ),
        (matrix, matrix),
        after=(mark,),
        moved=slots * 18 * order * order,
        flops=slots * 4 * order**3,
        grid=(slots,),
        limit=24,
    )

    below_low, above_high = gate((below_low, above_high), mark)
    far_low, far_high = both_ways(below_low, above_high)

    direction, _ = placed(table_first, plan_first[6:], far_first, direction)
    plan = half_plan(size_rest)
    direction, _ = placed(
        table_rest, plan[:6], [low, high, above_low, above_high, below_low, below_high], direction, (), 59
    )
    direction, _ = placed(table_rest, plan[6:], [far_low, far_high], direction, (), 59)
    return (new_left, new_right, direction)


def local(grads, owner, *others):
    position = jnp.arange(owner.shape[0], dtype=jnp.int32)
    same_owner = (owner[:, None] == owner[None, :]) & (position[None, :] < position[:, None])
    col_rank = jnp.sum(same_owner.astype(jnp.int32), axis=1)
    longest = jnp.sum(((col_rank == 4) | (col_rank == 8)).astype(jnp.int32))
    return lax.cond(
        longest <= 48,
        functools.partial(step, 48),
        functools.partial(step, 56),
        grads,
        owner,
        col_rank,
        *others,
    )


def solution(mesh):
    placed = (
        P("rep", None, "fsdp", None),
        P(),
        P(("rep", "fsdp"), None, None),
        P(("rep", "fsdp"), None, None),
        P(("rep", "fsdp"), None, None),
        P(("rep", "fsdp"), None, None),
    )
    return jax.shard_map(
        local,
        mesh=mesh,
        in_specs=placed,
        out_specs=(
            P(("rep", "fsdp"), None, None),
            P(("rep", "fsdp"), None, None),
            P(None, "fsdp", None),
        ),
        check_vma=False,
    )
```

```python
import functools

import jax
import jax.numpy as jnp
from jax import lax
from jax.experimental import pallas as pl
from jax.experimental.pallas import tpu as pltpu
from jax.sharding import PartitionSpec as P

epsilon = 1e-06
decay_rate = 0.9

ANY = pl.BlockSpec(memory_space=pl.ANY)
HBM = pl.BlockSpec(memory_space=pltpu.HBM)
SMEM = pl.BlockSpec(memory_space=pltpu.SMEM)
VMEM = pl.BlockSpec(memory_space=pltpu.VMEM)
F32 = jnp.float32
MIB = 1024 * 1024


def cost(nbytes, flops=0):
    return pl.CostEstimate(flops=flops, bytes_accessed=nbytes, transcendentals=0)


def batched(count, read, write, batch=4):
    def some(i, _):
        pieces = [read(batch * i + lane) for lane in range(batch)]
        for lane in range(batch):
            write(batch * i + lane, pieces[lane])
        return 0

    lax.fori_loop(0, count // batch, some, 0)


def put(out, *where):
    def write(j, piece):
        out[(j, *where)] = piece.astype(out.dtype)

    return write


def lay_kernel(plan, table, rows, zeros):
    last = rows.shape[0] - 1
    for start, out in plan:

        def read(j, start=start):
            block = table[start + j]
            piece = rows[jnp.minimum(block, last)]
            return jnp.where(block <= last, piece, jnp.zeros_like(piece)) if zeros else piece

        batched(out.shape[0], read, put(out))


def second_kernel(got_low, got_high, low_rows, high_rows, low, high):
    for got, own, out in ((got_low, low_rows, low), (got_high, high_rows, high)):
        batched(
            out.shape[0],
            lambda j, got=got, own=own: own[j].astype(F32) + got[j].astype(F32),
            put(out),
        )


def second_whole_kernel(got_low, got_high, up_rows, down_rows, up, down):
    half = got_low.shape[0]

    def write_up(j, piece):
        up[half + j] = piece

    def write_down(j, piece):
        down[half + j] = piece.astype(down.dtype)

    batched(half, lambda j: up_rows[j].astype(F32) + got_low[j].astype(F32), put(up))
    batched(half, lambda j: up_rows[half + j], write_up)
    batched(half, lambda j: down_rows[j], put(down))
    batched(half, lambda j: down_rows[half + j].astype(F32) + got_high[j].astype(F32), write_down)


def third_first_kernel(own, up_low, up_high, down_low, down_high, out):
    half = up_low.shape[0]
    for first, from_up, from_down in ((0, up_low, down_low), (half, up_high, down_high)):

        def read(k, first=first, from_up=from_up, from_down=from_down):
            return own[first + k].astype(F32) + from_up[k].astype(F32) + from_down[k].astype(F32)

        def write(k, piece, first=first):
            out[first + k, 0] = piece.astype(out.dtype)

        batched(half, read, write)


def third_kernel(size, base, last, table, place, own, from_up, from_down, out):
    for part in range(out.shape[1]):
        batched(out.shape[0], lambda j: jnp.zeros(out.shape[2:], F32), put(out, part))
    count = lax.fori_loop(0, size, lambda j, n: n + jnp.where(table[j] <= last, 1, 0), 0, unroll=8)

    def some(i, _):
        entries = [jnp.minimum(4 * i + lane, count - 1) for lane in range(4)]
        totals = [own[j].astype(F32) + from_up[j].astype(F32) + from_down[j].astype(F32) for j in entries]
        for j, total in zip(entries, totals):
            where = place[table[j]]
            out[where & 31, (where >> 5) - base] = total.astype(out.dtype)
        return 0

    lax.fori_loop(0, (count + 3) // 4, some, 0)


def pack_kernel(half, base, last, table, place, returned, low, high):
    for first, out in ((0, low), (half, high)):

        def read(j, first=first):
            where = place[jnp.minimum(table[first + j], last)]
            return returned[where & 31, jnp.maximum((where >> 5) - base, 0)]

        batched(half, read, put(out))


def take_kernel(part, mixed, low, high):
    half = low.shape[0]
    batched(half, lambda j: mixed[j, part], put(low))
    batched(half, lambda j: mixed[half + j, part], put(high))


def place_kernel(plan, last, table, *refs):
    sources, out, sem = refs[: len(plan)], refs[-2], refs[-1]
    started = jnp.int32(0)
    for source, (start, count, shift) in zip(sources, plan):

        def one(j, n, source=source, start=start, shift=shift):
            block = table[start + j]

            @pl.when(block <= last)
            def _():
                pltpu.make_async_copy(source.at[shift + j], out.at[block], sem).start()

            return n + jnp.where(block <= last, 1, 0)

        started = lax.fori_loop(0, count, one, started, unroll=4)

    def done(_, n):
        pltpu.make_async_copy(sources[0].at[0], out.at[0], sem).wait()
        return n

    lax.fori_loop(0, started, done, 0)


def apply_kernel(held, left, right, shaped):
    order = left.shape[-1]
    block = held[...].reshape(order, order)
    applied = jnp.dot(left[0], block, preferred_element_type=F32).astype(jnp.bfloat16)
    product = jnp.dot(applied, right[0], preferred_element_type=F32)
    wide = block.astype(F32)
    count = order * order
    held_power = jnp.sum(wide * wide) / count
    power = jnp.sum(product * product) / count
    scale = jnp.sqrt((held_power + epsilon) / (power + epsilon))
    shaped[...] = (product * scale).astype(jnp.bfloat16).reshape(shaped.shape)


def gram_kernel(held_first, held_rest, left, right, new_left, new_right):
    order = left.shape[-1]
    block = jnp.where(pl.program_id(0) == 0, held_first[...], held_rest[...]).reshape(order, order)
    weight = (1.0 - decay_rate) / order
    left_gram = lax.dot_general(block, block, (((1,), (1,)), ((), ())), preferred_element_type=F32)
    right_gram = lax.dot_general(block, block, (((0,), (0,)), ((), ())), preferred_element_type=F32)
    new_left[0] = decay_rate * left[0] + weight * left_gram
    new_right[0] = decay_rate * right[0] + weight * right_gram


def step(size_rest, grads, owner, col_rank, factor_left, factor_right, precond_left, precond_right):
    rows = grads[0]
    blocks, band, width = rows.shape
    columns = lax.axis_size("fsdp")
    replicas = lax.axis_size("rep")
    my_rep = lax.axis_index("rep")
    slots = factor_left.shape[0]
    last = blocks - 1
    up_pairs = [(i, (i + 1) % replicas) for i in range(replicas)]
    down_pairs = [(i, (i - 1) % replicas) for i in range(replicas)]
    far_pairs = [(i, (i + 2) % replicas) for i in range(replicas)]

    position = jnp.arange(blocks, dtype=jnp.int32)
    earlier = position[None, :] < position[:, None]
    rep_of = col_rank % replicas
    local_slot = col_rank // replicas
    relative = (rep_of - my_rep) % replicas
    place = local_slot * columns + owner

    def listed(key, size):
        hits = key[None, :] == jnp.arange(size, dtype=jnp.int32)[:, None]
        return jnp.min(jnp.where(hits, position[None, :], blocks), axis=1)

    size_first = columns
    by_column = relative * columns + owner
    table_first = listed(jnp.where(local_slot == 0, by_column, -1), replicas * columns)

    def packed(member, size):
        same_list = (rep_of[:, None] == rep_of[None, :]) & member[None, :] & earlier
        in_list = jnp.sum(same_list.astype(jnp.int32), axis=1)
        return listed(jnp.where(member, relative * size + in_list, -1), replicas * size)

    table_rest = packed(local_slot > 0, size_rest)

    def piece(*count):
        return jax.ShapeDtypeStruct((*count, band, width), jnp.bfloat16)

    def nbytes(count):
        return count * band * width * 2

    token = jax.ShapeDtypeStruct((8, 128), F32)

    def call(kernel, results, operands, specs, out_specs, scratch=(), after=(), moved=0, flops=0, grid=None, aliases=None, limit=16):
        count, late = len(operands), len(after)
        n_out = len(results)
        small = pl.BlockSpec((8, 128), lambda *_: (0, 0)) if grid else VMEM

        def body(*refs):
            outs = refs[count + late : count + late + n_out]
            mark = refs[count + late + n_out]
            mark[...] = jnp.zeros_like(mark)
            kernel(*refs[:count], *outs, *refs[count + late + n_out + 1 :])

        extra = {} if grid is None else {"grid": grid}
        return pl.pallas_call(
            body,
            out_shape=(*results, token),
            in_specs=list(specs) + [ANY] * late,
            out_specs=(*out_specs, small),
            scratch_shapes=list(scratch),
            input_output_aliases=aliases or {},
            compiler_params=pltpu.CompilerParams(vmem_limit_bytes=limit * MIB),
            cost_estimate=pl.CostEstimate(flops=flops, bytes_accessed=moved, transcendentals=0),
            **extra,
        )(*operands, *after)

    def tip(x):
        return x[0, :16, :128]

    def gate(values, *marks):
        shapes = tuple(jax.ShapeDtypeStruct(v.shape, v.dtype) for v in values)
        return pl.pallas_call(
            lambda *refs: None,
            out_shape=shapes,
            in_specs=[ANY] * (len(values) + len(marks)),
            out_specs=(ANY,) * len(values),
            input_output_aliases={i: i for i in range(len(values))},
        )(*values, *marks)

    def both_ways(up, down):
        return lax.ppermute(up, "rep", up_pairs), lax.ppermute(down, "rep", down_pairs)

    def half_plan(size):
        return [(relative * size + first, size // 2, 0) for relative in (0, 1, 3, 2) for first in (0, size // 2)]

    def tip(x):
        return x[0, :16, :128]

    def both_ways(up, down):
        return lax.ppermute(up, "rep", up_pairs), lax.ppermute(down, "rep", down_pairs)

    def half_plan(size):
        return [(relative * size + first, size // 2, 0) for relative in (0, 1, 3, 2) for first in (0, size // 2)]

    def far_plan(size):
        half = size // 2
        return [(2 * size, half, 0), (2 * size + half, half, 0)]

    def exchange(x):
        return lax.all_to_all(x, "fsdp", split_axis=0, concat_axis=0, tiled=True)

    def applied(held, base, depth, order_after, moved=0):
        strip = pl.BlockSpec((columns, 1, band, width), lambda s: (0, s, 0, 0))
        matrix = pl.BlockSpec((1, order, order), lambda s: (s + base, 0, 0))
        return call(
            apply_kernel,
            (piece(columns, depth),),
            (held, precond_left, precond_right),
            (strip, matrix, matrix),
            (strip,),
            after=order_after,
            moved=moved,
            grid=(depth,),
            limit=16,
        )

    def placed(table, plan, sources, out, after=(), limit=16):
        operands = (table, *sources) if out is None else (table, *sources, out)
        specs = [SMEM] + [VMEM] * len(sources) + ([] if out is None else [HBM])

        def kernel(*refs):
            place_kernel(plan, last, *refs[: 1 + len(plan)], *refs[-2:])

        return call(
            kernel,
            (piece(blocks),),
            operands,
            specs,
            (HBM,),
            [pltpu.SemaphoreType.DMA],
            after,
            nbytes(2 * sum(p[1] for p in plan)),
            aliases=None if out is None else {1 + len(sources): 0},
            limit=limit,
        )

    order = factor_left.shape[1]
    depth_rest = slots - 1
    half_first, half_rest = size_first // 2, size_rest // 2
    def lay(table, size, parts, marks, zeros):
        def kernel(table, rows, *outs):
            lay_kernel([(p[0] * size + p[1], out) for p, out in zip(parts, outs)], table, rows, zeros)

        return call(
            kernel,
            tuple(piece(p[-1]) for p in parts),
            (table, rows),
            (SMEM, VMEM),
            (VMEM,) * len(parts),
            after=marks,
            moved=nbytes(2 * sum(p[-1] for p in parts)),
        )

    low_first, high_first, plain_up, plain_down, near_low, near_high, mine_first, mark = lay(
        table_first,
        size_first,
        [
            (2, 0, half_first),
            (2, half_first, half_first),
            (1, half_first, half_first),
            (3, 0, half_first),
            (1, 0, half_first),
            (3, half_first, half_first),
            (0, 0, size_first),
        ],
        (),
        True,
    )
    got_low_first, got_high_first = both_ways(low_first, high_first)
    up_high, down_low = both_ways(plain_up, plain_down)
    low, high, mark = call(
        second_kernel,
        (piece(half_first), piece(half_first)),
        (got_low_first, got_high_first, near_low, near_high),
        (VMEM,) * 4,
        (VMEM, VMEM),
        moved=nbytes(3 * size_first),
    )
    up_low, down_high = both_ways(low, high)
    low_rest, high_rest, up_rest, down_rest, mine_rest, mark = lay(
        table_rest,
        size_rest,
        [(2, 0, half_rest), (2, half_rest, half_rest), (1, 0, size_rest), (3, 0, size_rest), (0, 0, size_rest)],
        (mark,),
        False,
    )
    sent_first, mark = call(
        third_first_kernel,
        (piece(columns, 1),),
        (mine_first, up_low, up_high, down_low, down_high),
        (VMEM,) * 5,
        (VMEM,),
        after=(mark,),
        moved=nbytes(4 * size_first),
    )
    low_rest, high_rest = gate((low_rest, high_rest), mark)
    got_low_rest, got_high_rest = both_ways(low_rest, high_rest)
    held_first = exchange(sent_first)
    up, down, mark = call(
        second_whole_kernel,
        (piece(size_rest), piece(size_rest)),
        (got_low_rest, got_high_rest, up_rest, down_rest),
        (VMEM,) * 4,
        (VMEM, VMEM),
        after=(mark,),
        moved=nbytes(3 * size_rest),
    )
    from_up, from_down = both_ways(up, down)
    shaped_first, mark = applied(held_first, 0, 1, (mark,))
    back_first = exchange(shaped_first)
    own_low, own_high, mark = call(
        functools.partial(take_kernel, 0),
        (piece(half_first), piece(half_first)),
        (back_first,),
        (VMEM,),
        (VMEM, VMEM),
        moved=nbytes(2 * size_first),
    )
    sent_rest, _ = call(
        functools.partial(third_kernel, size_rest, 1, last),
        (piece(columns, depth_rest),),
        (table_rest, place, mine_rest, from_up, from_down),
        (SMEM, SMEM, VMEM, VMEM, VMEM),
        (VMEM,),
        moved=nbytes(5 * size_rest),
    )
    [sent_rest] = gate((sent_rest,), mark)
    held_rest = exchange(sent_rest)
    below_low, above_high = both_ways(own_low, own_high)
    below_high, above_low = both_ways(own_high, own_low)
    far_low, far_high = both_ways(below_low, above_high)
    far_first = [far_low, far_high]
    shaped_rest, mark = applied(held_rest, 1, depth_rest, (tip(below_low), tip(above_high)))
    back_rest = exchange(shaped_rest)
    plan_first = half_plan(size_first)
    direction, mark_placed = placed(
        table_first,
        plan_first[:6],
        [own_low, own_high, above_low, above_high, below_low, below_high],
        None,
    )
    low, high, mark = call(
        functools.partial(pack_kernel, half_rest, 1, last),
        (piece(half_rest), piece(half_rest)),
        (table_rest, place, back_rest),
        (SMEM, SMEM, VMEM),
        (VMEM, VMEM),
        after=(mark_placed, tip(far_first[0]), tip(far_first[1])),
        moved=nbytes(2 * size_rest),
    )
    below_low, above_high = both_ways(low, high)
    below_high, above_low = both_ways(high, low)
    matrix = pl.BlockSpec((1, order, order), lambda s: (s, 0, 0))
    new_left, new_right, mark = call(
        gram_kernel,
        (
            jax.ShapeDtypeStruct(factor_left.shape, F32),
            jax.ShapeDtypeStruct(factor_right.shape, F32),
        ),
        (held_first, held_rest, factor_left, factor_right),
        (
            pl.BlockSpec((columns, 1, band, width), lambda s: (0, 0, 0, 0)),
            pl.BlockSpec((columns, 1, band, width), lambda s: (0, jnp.maximum(s - 1, 0), 0, 0)),
            matrix,
            matrix,
        ),
        (matrix, matrix),
        after=(mark,),
        moved=slots * 18 * order * order,
        flops=slots * 4 * order**3,
        grid=(slots,),
        limit=24,
    )

    below_low, above_high = gate((below_low, above_high), mark)
    far_low, far_high = both_ways(below_low, above_high)

    direction, _ = placed(table_first, plan_first[6:], far_first, direction)
    plan = half_plan(size_rest)
    direction, _ = placed(
        table_rest, plan[:6], [low, high, above_low, above_high, below_low, below_high], direction, (), 59
    )
    direction, _ = placed(table_rest, plan[6:], [far_low, far_high], direction, (), 61)
    return (new_left, new_right, direction)


def local(grads, owner, *others):
    position = jnp.arange(owner.shape[0], dtype=jnp.int32)
    same_owner = (owner[:, None] == owner[None, :]) & (position[None, :] < position[:, None])
    col_rank = jnp.sum(same_owner.astype(jnp.int32), axis=1)
    longest = jnp.sum(((col_rank == 4) | (col_rank == 8)).astype(jnp.int32))
    return lax.cond(
        longest <= 48,
        functools.partial(step, 48),
        functools.partial(step, 56),
        grads,
        owner,
        col_rank,
        *others,
    )


def solution(mesh):
    placed = (
        P("rep", None, "fsdp", None),
        P(),
        P(("rep", "fsdp"), None, None),
        P(("rep", "fsdp"), None, None),
        P(("rep", "fsdp"), None, None),
        P(("rep", "fsdp"), None, None),
    )
    return jax.shard_map(
        local,
        mesh=mesh,
        in_specs=placed,
        out_specs=(
            P(("rep", "fsdp"), None, None),
            P(("rep", "fsdp"), None, None),
            P(None, "fsdp", None),
        ),
        check_vma=False,
    )
```
